32 devices in a mesh: lon: 8 (over z, y), lat: 4 (over x, core).
Axes of the slice: x: 2, y: 2, z: 4, core: 2. Of those that a mesh axis runs over, the one named last changes fastest.
Arguments:
- control: float32 [80, 128, 1024], P(None, 'lat', 'lon'), may hold values from -6 to 6
- diffusivity: float32 [128, 1024], P('lat', 'lon'), may hold values from 0.02 to 0.12
- land_mask: int32 [128, 1024], P('lat', 'lon'), may hold values 0 or 1
- innovations: float32 [4, 80, 1024], P('lat', None, 'lon'), may hold values from -6 to 6
- obs_sigma: float32 [4, 80, 1024], P('lat', None, 'lon'), may hold values from 0.5 to 2
- obs_row: int32 [4, 1024], P('lat', 'lon'), may hold values from 0 to 31
- obs_col: int32 [4, 1024], P('lat', 'lon'), may hold values from 0 to 127
- obs_frac: float32 [4, 2, 1024], P('lat', None, 'lon'), may hold values from 0 to 1
- obs_counts: int32 [4, 8], P('lat', 'lon'), may hold values from 32 to 128, as said below
Outputs:
- obs_gradient: float32 [80, 128, 1024], P(None, 'lat', 'lon')
- departures: float32 [4, 80, 1024], P('lat', None, 'lon')
The draws below stay inside these ranges and needn't reach their ends.
Inputs may be any that keep to these rules, and one draw needn't show every extreme that they name: `obs_counts`: every tile holds between 32 and 128 live profiles in its first slots; some tile holds exactly 128.
All inputs are finite; a program needn't handle non-finite values. No bound on the sum of `land_mask` on one device may be relied on, other than what follows from the above.
Results may differ from the reference program's by a relative error of at most 0.00002.
Values sent between devices are 32-bit elements; how exact they have to be, the bound alone decides.
A program may use at most 64 MiB of HBM per device.

```python
import math
import jax
import jax.numpy as jnp
from jax import lax

TX = 128
TY = 32
VARS = 2
LEV = 40
OBS = 128
NX = 1024
NY = 128
N_LON = 8
N_LAT = 4


def draw_obs_counts(key, part):
    first_key, second_key = jax.random.split(jax.random.fold_in(key, 17))
    counts = jax.random.randint(first_key, (N_LAT, N_LON), OBS // 4, OBS + 1)
    chosen = jax.random.randint(second_key, (), 0, N_LAT * N_LON)
    places = jnp.arange(N_LAT * N_LON).reshape(N_LAT, N_LON)
    return jnp.where(places == chosen, OBS, counts).astype(jnp.int32)


def with_ends(values, stream_key, low, largest):
    index_at = [jax.random.randint(jax.random.fold_in(stream_key, axis), (), 0, length) for axis, length in enumerate(values.shape)]
    longest = values.shape.index(max(values.shape))
    beside = index_at[:longest] + [(index_at[longest] + 1) % values.shape[longest]] + index_at[longest + 1:]
    return values.at[tuple(index_at)].set(low).at[tuple(beside)].set(largest)


def level_of(stream_key, extent, cuts, least, top_value):
    def one(position, parts):
        steps = jax.random.uniform(jax.random.fold_in(jax.random.fold_in(stream_key, 6), position), (parts,), jnp.float32, least / len(cuts), top_value / len(cuts))
        return jnp.repeat(jnp.exp(steps), extent[position] // parts).reshape((-1,) + (1,) * (len(extent) - position - 1))

    factor_of = one(*cuts[0])
    for cut in cuts[1:]:
        factor_of = factor_of * one(*cut)
    return factor_of


def normal_values(stream_key, dims, scale, reach, shards=(), kind=jnp.bfloat16):
    drawn = scale * jax.random.normal(stream_key, dims, jnp.float32)
    if shards:
        drawn = drawn * level_of(stream_key, dims, shards, -0.22, 0.18)
    return jnp.clip(drawn, -reach, reach).astype(kind)


def setup_inputs(seed: int = 0) -> dict:
    splits = jax.random.split(jax.random.key(seed), 10)
    return {
        "control": normal_values(splits[0], (VARS * LEV, NY, NX), 1.0, 6.0, ((1, 4), (2, 8)), jnp.float32),
        "diffusivity": jnp.clip(jnp.exp(math.log(0.12) - 1.7917595 * jax.random.uniform(splits[1], (NY, NX), jnp.float32) ** level_of(splits[1], (NY, NX), ((0, 4), (1, 8)), -0.2, 0.2)), 0.02, 0.12),
        "land_mask": with_ends((jax.random.randint(splits[2], (NY, NX), 0, 10) < 7).astype(jnp.int32), jax.random.fold_in(splits[2], 1), 0, 1),
        "innovations": normal_values(splits[3], (N_LAT, VARS * LEV, N_LON * OBS), 1.0, 6.0, ((0, 4), (2, 8)), jnp.float32),
        "obs_sigma": jnp.clip(jnp.exp(math.log(2.0) - 1.3862944 * jax.random.uniform(splits[4], (N_LAT, VARS * LEV, N_LON * OBS), jnp.float32) ** level_of(splits[4], (N_LAT, VARS * LEV, N_LON * OBS), ((0, 4), (2, 8)), -0.2, 0.2)), 0.5, 2.0),
        "obs_row": with_ends(jax.random.randint(splits[5], (N_LAT, N_LON * OBS), 0, TY), jax.random.fold_in(splits[5], 1), 0, TY - 1).astype(jnp.int32),
        "obs_col": with_ends(jax.random.randint(splits[6], (N_LAT, N_LON * OBS), 0, TX), jax.random.fold_in(splits[6], 1), 0, TX - 1).astype(jnp.int32),
        "obs_frac": jnp.clip(1.0 * jax.random.uniform(splits[7], (N_LAT, 2, N_LON * OBS), jnp.float32) ** level_of(splits[7], (N_LAT, 2, N_LON * OBS), ((0, 4), (2, 8)), -0.2, 0.2), 0.0, 1.0),
        "obs_counts": draw_obs_counts(jax.random.fold_in(splits[9], 71), 0),
    }


def window(array, offset_y, offset_x):
    return array[..., 1 + offset_y: array.shape[-2] - 1 + offset_y, 1 + offset_x: array.shape[-1] - 1 + offset_x]


def diffuse(padded, kappa_pad, mask_pad):
    center = window(padded, 0, 0)
    kappa_mid = window(kappa_pad, 0, 0)
    mask_mid = window(mask_pad, 0, 0)
    result = center
    for offset_y, offset_x in ((0, 1), (0, -1), (1, 0), (-1, 0)):
        weight = 0.5 * (kappa_mid + window(kappa_pad, offset_y, offset_x)) * mask_mid * window(mask_pad, offset_y, offset_x)
        result = result + weight * (window(padded, offset_y, offset_x) - center)
    return result


def wrap_pad(field):
    joined = jnp.concatenate([field[:, -1:], field, field[:, :1]], axis=1)
    return jnp.pad(joined, ((1, 1), (0, 0)))


def reference(control, diffusivity, land_mask, innovations, obs_sigma, obs_row, obs_col, obs_frac, obs_counts):
    mask_float = land_mask.astype(jnp.float32)
    kappa_pad = wrap_pad(diffusivity)
    mask_pad = wrap_pad(mask_float)

    def smooth(field):
        for repeat in range(2):
            field = diffuse(wrap_pad(field), kappa_pad, mask_pad)
        return field

    lat_tile = jnp.broadcast_to(jnp.arange(N_LAT, dtype=jnp.int32)[:, None], obs_row.shape)
    column = jnp.broadcast_to(jnp.arange(N_LON * OBS, dtype=jnp.int32)[None, :], obs_row.shape)
    lon_tile = column // OBS
    slot_index = column % OBS
    grid_row = lat_tile * TY + obs_row + 1
    grid_col = lon_tile * TX + obs_col + 1
    valid = (slot_index < obs_counts[lat_tile, lon_tile]).astype(jnp.float32)
    frac_y = obs_frac[:, 0, :]
    frac_x = obs_frac[:, 1, :]
    stencil = ((0, 0, (1.0 - frac_y) * (1.0 - frac_x)), (0, 1, (1.0 - frac_y) * frac_x),
               (1, 0, frac_y * (1.0 - frac_x)), (1, 1, frac_y * frac_x))

    def level(inputs):
        field, innov, sigma = inputs
        state = smooth(field)
        padded = wrap_pad(state)
        sample = jnp.zeros_like(innov)
        for offset_y, offset_x, weight in stencil:
            sample = sample + weight * padded[grid_row + offset_y, grid_col + offset_x]
        departure = valid * (sample - innov)
        weighted = departure / (sigma * sigma)
        adjoint = jnp.zeros_like(padded)
        for offset_y, offset_x, weight in stencil:
            adjoint = adjoint.at[grid_row + offset_y, grid_col + offset_x].add(weight * weighted)
        inner = adjoint[1:-1, 1:-1]
        inner = inner.at[:, 0].add(adjoint[1:-1, -1])
        return smooth(inner), departure

    grads, departs = lax.map(level, (control, jnp.moveaxis(innovations, 1, 0), jnp.moveaxis(obs_sigma, 1, 0)))
    return grads, jnp.moveaxis(departs, 0, 1)
```

```python
import functools

import jax
import jax.numpy as jnp
from jax import lax
from jax.experimental import pallas as pl
from jax.experimental.pallas import tpu as pltpu
from jax.sharding import PartitionSpec as P

F32 = jnp.float32
BF16 = jnp.bfloat16
PACK = 16
SLOT = 8
EDGE = 4
MESH = pl.DeviceIdType.MESH


def kernel(
    levels,
    control, diffusivity, land_mask, innovations, sigma, obs_row, obs_col, frac, counts,
    gradient, departures,
    coeff, weights, strip_weights, hot_in, hot_out, work, adjoint,
    pack, rows_up, rows_dn, prow_up, prow_dn,
    pack_e, pack_w, got_up, got_dn, pgot_up, pgot_dn,
    bpack, brow_up, brow_dn, bprow_up, bprow_dn,
    bpack_e, bpack_w, bgot_up, bgot_dn, bpgot_up, bpgot_dn,
    send_sem, recv_sem, bsend_sem, brecv_sem,
):
    ty, tx = control.shape[1], control.shape[2]
    ext = ty + 8
    groups = levels // PACK
    lon, lat = lax.axis_index("lon"), lax.axis_index("lat")
    n_lon, n_lat = lax.axis_size("lon"), lax.axis_size("lat")
    east, west = lax.rem(lon + 1, n_lon), lax.rem(lon + n_lon - 1, n_lon)
    has_up, has_dn = lat < n_lat - 1, lat > 0
    columns = (lon, east, west)

    barrier = pltpu.get_barrier_semaphore()

    def greet(x, y):
        pl.semaphore_signal(barrier, inc=1, device_id={"lon": x, "lat": y}, device_id_type=MESH)

    greet(east, lat)
    greet(west, lat)

    @pl.when(has_up)
    def _():
        for x in columns:
            greet(x, lat + 1)

    @pl.when(has_dn)
    def _():
        for x in columns:
            greet(x, lat - 1)

    def copy(src, dst, sends, recvs, index, x, y):
        return pltpu.make_async_remote_copy(
            src_ref=src, dst_ref=dst, send_sem=sends.at[index], recv_sem=recvs.at[index],
            device_id={"lon": x, "lat": y}, device_id_type=MESH,
        )

    place = (0, 2, 1)

    lane = lax.broadcasted_iota(jnp.int32, (ext, tx), 1)
    slot = lax.rem(lane, SLOT)
    sub8 = lax.broadcasted_iota(jnp.int32, (8, tx), 0)

    coeff[0] = diffusivity[...]
    coeff[1] = land_mask[...].astype(F32)
    rows_up[0:levels] = control[:, ty - EDGE : ty, :]
    rows_dn[0:levels] = control[:, 0:EDGE, :]
    rows_up[levels : levels + 2] = coeff[:, ty - EDGE : ty, :]
    rows_dn[levels : levels + 2] = coeff[:, 0:EDGE, :]

    lane_t = lane[0:ty]

    def pack_group(g, carry):
        acc = jnp.zeros((ty, tx), F32)
        for p in range(PACK):
            x = control[g * PACK + p]
            acc = jnp.where(lane_t // SLOT == p, pltpu.roll(x, SLOT * p + 2, 1), acc)
        pack[g] = acc
        return carry

    lax.fori_loop(0, groups, pack_group, 0)
    for k in range(2):
        base = jnp.where(lane_t < SLOT, pltpu.roll(coeff[k], 2, 1), 0.0)
        width = SLOT
        while width < tx:
            base = base + pltpu.roll(base, width, 1)
            width *= 2
        pack[groups + k] = base
    prow_up[...] = pack[:, ty - EDGE : ty, :]
    prow_dn[...] = pack[:, 0:EDGE, :]

    @pl.when(jnp.logical_and(has_up, has_dn))
    def _():
        pl.semaphore_wait(barrier, 8)

    @pl.when(jnp.logical_not(jnp.logical_and(has_up, has_dn)))
    def _():
        pl.semaphore_wait(barrier, 5)

    side_copies = (
        copy(pack, pack_w, send_sem, recv_sem, 0, east, lat),
        copy(pack, pack_e, send_sem, recv_sem, 1, west, lat),
    )

    def up_copies():
        return [copy(rows_up, got_dn, send_sem, recv_sem, 2, lon, lat + 1)] + [
            copy(prow_up, pgot_dn.at[place[i]], send_sem, recv_sem, 4 + i, columns[i], lat + 1)
            for i in range(3)
        ]

    def dn_copies():
        return [copy(rows_dn, got_up, send_sem, recv_sem, 3, lon, lat - 1)] + [
            copy(prow_dn, pgot_up.at[place[i]], send_sem, recv_sem, 7 + i, columns[i], lat - 1)
            for i in range(3)
        ]

    for c in side_copies:
        c.start()

    @pl.when(has_up)
    def _():
        for c in up_copies():
            c.start()

    @pl.when(has_dn)
    def _():
        for c in dn_copies():
            c.start()

    col = obs_col[...]
    row = obs_row[...]
    cell = lax.broadcasted_iota(jnp.int32, (tx, tx), 0)
    kind = lax.rem(cell, SLOT)

    def hot(wanted):
        return jnp.concatenate(
            [jnp.where(col == wanted, 1.0, 0.0), jnp.where(col + 1 == wanted, 1.0, 0.0)], axis=1
        ).astype(BF16)

    main_hot = hot(cell)
    hot_in[0:tx] = main_hot
    hot_in[tx : 2 * tx] = hot(jnp.where(kind == 2, tx, -9))
    chosen = jnp.where(
        kind < 3, tx - 2 + kind, jnp.where(kind == 5, 0, jnp.where(kind == 6, 1, jnp.where(kind == 7, 0, -9)))
    )
    hot_out[0:tx] = main_hot
    hot_out[tx : 2 * tx] = hot(chosen)

    frac_y = frac[0, 0:1, :]
    frac_x = frac[0, 1:2, :]
    line = lax.broadcasted_iota(jnp.int32, (ext, tx), 0)
    row_weight = jnp.where(line == row, 1.0 - frac_y, 0.0) + jnp.where(line == row + 1, frac_y, 0.0)
    row_weight = jnp.where(jnp.logical_and(line == ty, lat == n_lat - 1), 0.0, row_weight)
    live = lax.broadcasted_iota(jnp.int32, (PACK, tx), 1) < counts[0, 0]

    for c in side_copies:
        c.wait()

    @pl.when(has_up)
    def _():
        for c in up_copies():
            c.wait_send()
        for c in dn_copies():
            c.wait_recv()

    @pl.when(has_dn)
    def _():
        for c in dn_copies():
            c.wait_send()
        for c in up_copies():
            c.wait_recv()

    @pl.when(jnp.logical_not(has_up))
    def _():
        got_up[...] = jnp.zeros_like(got_up)
        pgot_up[...] = jnp.zeros_like(pgot_up)

    @pl.when(jnp.logical_not(has_dn))
    def _():
        got_dn[...] = jnp.zeros_like(got_dn)
        pgot_dn[...] = jnp.zeros_like(pgot_dn)

    def strip_of(k):
        own = jnp.concatenate([pack[k], pgot_up[0, k], pgot_dn[0, k]], axis=0)
        e = jnp.concatenate([pack_e[k], pgot_up[1, k], pgot_dn[1, k]], axis=0)
        w = jnp.concatenate([pack_w[k], pgot_up[2, k], pgot_dn[2, k]], axis=0)
        far = jnp.where(slot == 7, pltpu.roll(own, 5, 1), pltpu.roll(w, 5, 1))
        return jnp.where(slot < 2, own, jnp.where(slot < 5, e, far))

    def edge_of(strip):
        return jnp.where(slot == 2, strip, pltpu.roll(strip, tx - 3, 1))

    def around(x, fill):
        left, right = pltpu.roll(x, 1, 1), pltpu.roll(x, tx - 1, 1)
        if fill is not None:
            left = jnp.where(lane == 0, fill, left)
            right = jnp.where(lane == tx - 1, fill, right)
        return left, right, pltpu.roll(x, 1, 0), pltpu.roll(x, ext - 1, 0)

    def fill_of(edge, p):
        return pltpu.roll(edge, (tx - 3 - SLOT * p) % tx, 1)

    def make_weights(dst, kappa, mask, kappas, masks):
        total = jnp.zeros_like(kappa)
        for i in range(4):
            w = 0.5 * (kappa + kappas[i]) * mask * masks[i]
            dst[i] = w
            total = total + w
        dst[4] = 1.0 - total

    kappa_strip, mask_strip = strip_of(groups), strip_of(groups + 1)
    make_weights(
        strip_weights, kappa_strip, mask_strip, around(kappa_strip, None), around(mask_strip, None)
    )
    kappa = jnp.concatenate([coeff[0], got_up[levels], got_dn[levels]], axis=0)
    mask = jnp.concatenate([coeff[1], got_up[levels + 1], got_dn[levels + 1]], axis=0)
    make_weights(
        weights, kappa, mask,
        around(kappa, fill_of(edge_of(kappa_strip), 0)),
        around(mask, fill_of(edge_of(mask_strip), 0)),
    )

    def diffuse(x, fill, w):
        near = around(x, fill)
        out = w[4] * x
        for i in range(4):
            out = out + w[i] * near[i]
        return out

    def parts(x):
        a = x.astype(BF16)
        rest = x - a.astype(F32)
        b = rest.astype(BF16)
        return a, b, (rest - b.astype(F32)).astype(BF16)

    def dot(x, y, dims):
        total = None
        for part in parts(x):
            one = lax.dot_general(part, y, (dims, ((), ())), preferred_element_type=F32)
            total = one if total is None else total + one
        return total

    def back_sides(g):
        return (
            copy(bpack.at[g], bpack_w.at[g], bsend_sem, brecv_sem, g * 10, east, lat),
            copy(bpack.at[g], bpack_e.at[g], bsend_sem, brecv_sem, g * 10 + 1, west, lat),
        )

    def back_up(g):
        mine = pl.ds(g * PACK, PACK)
        return [copy(brow_up.at[mine], bgot_dn.at[mine], bsend_sem, brecv_sem, g * 10 + 2, lon, lat + 1)] + [
            copy(bprow_up.at[g], bpgot_dn.at[place[i], g], bsend_sem, brecv_sem, g * 10 + 4 + i, columns[i], lat + 1)
            for i in range(3)
        ]

    def back_dn(g):
        mine = pl.ds(g * PACK, PACK)
        return [copy(brow_dn.at[mine], bgot_up.at[mine], bsend_sem, brecv_sem, g * 10 + 3, lon, lat - 1)] + [
            copy(bprow_dn.at[g], bpgot_up.at[place[i], g], bsend_sem, brecv_sem, g * 10 + 7 + i, columns[i], lat - 1)
            for i in range(3)
        ]

    def forward(g, carry):
        strip0 = strip_of(g)
        edge0 = edge_of(strip0)
        strip1 = diffuse(strip0, None, strip_weights)
        edge1 = edge_of(strip1)
        strip2 = diffuse(strip1, None, strip_weights)
        for p in range(PACK):
            level = g * PACK + p
            x = jnp.concatenate([control[level], got_up[level], got_dn[level]], axis=0)
            x = diffuse(x, fill_of(edge0, p), weights)
            x = diffuse(x, fill_of(edge1, p), weights)
            work[p, :, 0:tx] = x
            work[p, :, tx : 2 * tx] = jnp.where(lane // SLOT == p, strip2, 0.0)
        picked = dot(work[...].reshape(PACK * ext, 2 * tx), hot_in[...], ((1,), (0,)))
        mixed = picked[:, 0:tx] * (1.0 - frac_x) + picked[:, tx : 2 * tx] * frac_x
        sample = jnp.sum(mixed.reshape(PACK, ext, tx) * row_weight[None], axis=1)
        mine = pl.ds(g * PACK, PACK)
        departure = jnp.where(live, sample - innovations[0, mine, :], 0.0)
        departures[0, mine, :] = departure
        s = sigma[0, mine, :]
        weighted = departure / (s * s)
        spread = weighted[:, None, :] * row_weight[None]
        work[:, :, 0:tx] = spread * (1.0 - frac_x)[None]
        work[:, :, tx : 2 * tx] = spread * frac_x[None]
        field = dot(work[...].reshape(PACK * ext, 2 * tx), hot_out[...], ((1,), (1,)))
        adjoint[mine] = field[:, 0:tx].reshape(PACK, ext, tx)
        sides = field[:, tx : 2 * tx].reshape(PACK, ext, tx)
        acc = sides[0]
        for p in range(1, PACK):
            acc = jnp.where(lane // SLOT == p, sides[p], acc)
        bpack[g] = acc
        brow_up[mine] = adjoint[mine, ty - 3 : ty + 1, :]
        brow_dn[mine] = adjoint[mine, 0:EDGE, :]
        bprow_up[g] = bpack[g, ty - 3 : ty + 1, :]
        bprow_dn[g] = bpack[g, 0:EDGE, :]
        for c in back_sides(g):
            c.start()

        @pl.when(has_up)
        def _():
            for c in back_up(g):
                c.start()

        @pl.when(has_dn)
        def _():
            for c in back_dn(g):
                c.start()

        return carry

    lax.fori_loop(0, groups, forward, 0)

    @pl.when(jnp.logical_not(has_up))
    def _():
        bgot_up[...] = jnp.zeros_like(bgot_up)
        bpgot_up[...] = jnp.zeros_like(bpgot_up)

    @pl.when(jnp.logical_not(has_dn))
    def _():
        bgot_dn[...] = jnp.zeros_like(bgot_dn)
        bpgot_dn[...] = jnp.zeros_like(bpgot_dn)

    def with_rows(x, above, below):
        zero = jnp.zeros((EDGE, tx), F32)
        low = pltpu.roll(jnp.concatenate([zero, below], axis=0), 1, 0)
        first = x[0:8] + jnp.where(sub8 == 0, low, 0.0)
        last = x[ty:ext] + jnp.where(sub8 > 4, low, jnp.concatenate([above, zero], axis=0))
        return jnp.concatenate([first, x[8:ty], last], axis=0)

    def backward(g, carry):
        for c in back_sides(g):
            c.wait()

        @pl.when(has_up)
        def _():
            for c in back_up(g):
                c.wait_send()
            for c in back_dn(g):
                c.wait_recv()

        @pl.when(has_dn)
        def _():
            for c in back_dn(g):
                c.wait_send()
            for c in back_up(g):
                c.wait_recv()

        own = with_rows(bpack[g], bpgot_up[0, g], bpgot_dn[0, g])
        e = with_rows(bpack_e[g], bpgot_up[1, g], bpgot_dn[1, g])
        w = with_rows(bpack_w[g], bpgot_up[2, g], bpgot_dn[2, g])
        from_e = pltpu.roll(e, tx - 3, 1)
        from_w = pltpu.roll(w, 5, 1)
        strip = jnp.where(jnp.logical_or(slot < 3, slot == 7), own, 0.0)
        strip = strip + jnp.where(jnp.logical_or(slot == 2, slot == 3), from_e, 0.0)
        strip = strip + jnp.where(slot > 4, from_w, 0.0)
        first_col = jnp.where(slot == 7, from_w, 0.0)
        edge0 = edge_of(strip)
        edge1 = edge_of(diffuse(strip, None, strip_weights))
        for p in range(PACK):
            level = g * PACK + p
            x = with_rows(adjoint[level], bgot_up[level], bgot_dn[level])
            extra = pltpu.roll(first_col, (tx - 7 - SLOT * p) % tx, 1)
            x = x + jnp.where(lane == 0, extra, 0.0)
            x = diffuse(x, fill_of(edge0, p), weights)
            x = diffuse(x, fill_of(edge1, p), weights)
            gradient[level] = x[0:ty]
        return carry

    lax.fori_loop(0, groups, backward, 0)


def on_device(
    control, diffusivity, land_mask, innovations, obs_sigma, obs_row, obs_col, obs_frac, obs_counts
):
    levels, ty, tx = control.shape
    ext = ty + 8
    groups = levels // PACK
    vmem = pl.BlockSpec(memory_space=pltpu.VMEM)
    smem = pl.BlockSpec(memory_space=pltpu.SMEM)

    def buf(*shape, dtype=F32):
        return pltpu.VMEM(shape, dtype)

    scratch = [
        buf(2, ty, tx), buf(5, ext, tx), buf(5, ext, tx),
        buf(2 * tx, 2 * tx, dtype=BF16), buf(2 * tx, 2 * tx, dtype=BF16),
        buf(PACK, ext, 2 * tx), buf(levels, ext, tx),
        buf(groups + 2, ty, tx),
        buf(levels + 2, EDGE, tx), buf(levels + 2, EDGE, tx),
        buf(groups + 2, EDGE, tx), buf(groups + 2, EDGE, tx),
        buf(groups + 2, ty, tx), buf(groups + 2, ty, tx),
        buf(levels + 2, EDGE, tx), buf(levels + 2, EDGE, tx),
        buf(3, groups + 2, EDGE, tx), buf(3, groups + 2, EDGE, tx),
        buf(groups, ext, tx),
        buf(levels, EDGE, tx), buf(levels, EDGE, tx),
        buf(groups, EDGE, tx), buf(groups, EDGE, tx),
        buf(groups, ext, tx), buf(groups, ext, tx),
        buf(levels, EDGE, tx), buf(levels, EDGE, tx),
        buf(3, groups, EDGE, tx), buf(3, groups, EDGE, tx),
        pltpu.SemaphoreType.DMA((10,)), pltpu.SemaphoreType.DMA((10,)),
        pltpu.SemaphoreType.DMA((10 * groups,)), pltpu.SemaphoreType.DMA((10 * groups,)),
    ]
    return pl.pallas_call(
        functools.partial(kernel, levels),
        out_shape=(
            jax.ShapeDtypeStruct(control.shape, F32),
            jax.ShapeDtypeStruct(innovations.shape, F32),
        ),
        in_specs=[vmem] * 8 + [smem],
        out_specs=(vmem, vmem),
        scratch_shapes=scratch,
        compiler_params=pltpu.CompilerParams(
            collective_id=0, has_side_effects=True, vmem_limit_bytes=40 * 1024 * 1024
        ),
    )(control, diffusivity, land_mask, innovations, obs_sigma, obs_row, obs_col, obs_frac, obs_counts)


def solution(mesh):
    in_specs = (
        P(None, "lat", "lon"),
        P("lat", "lon"),
        P("lat", "lon"),
        P("lat", None, "lon"),
        P("lat", None, "lon"),
        P("lat", "lon"),
        P("lat", "lon"),
        P("lat", None, "lon"),
        P("lat", "lon"),
    )
    out_specs = (P(None, "lat", "lon"), P("lat", None, "lon"))
    return jax.shard_map(
        on_device, mesh=mesh, in_specs=in_specs, out_specs=out_specs, check_vma=False
    )
```

```python
import functools

import jax
import jax.numpy as jnp
from jax import lax
from jax.experimental import pallas as pl
from jax.experimental.pallas import tpu as pltpu
from jax.sharding import PartitionSpec as P

F32 = jnp.float32
BF16 = jnp.bfloat16
PACK = 16
SLOT = 8
EDGE = 4
MESH = pl.DeviceIdType.MESH


def kernel(
    levels,
    control_in, diffusivity_in, land_mask_in, innovations_in, sigma_in,
    obs_row_in, obs_col_in, frac_in, counts,
    gradient, departures,
    control, diffusivity, land_mask, innovations, sigma, obs_row, obs_col, frac, local_sem,
    coeff, weights, strip_weights, hot_in, hot_out, work, adjoint,
    pack, send_e, send_w, rows_up, rows_dn,
    from_w, from_e, pack_e, pack_w, got_up, got_dn, pgot_up, pgot_dn,
    bpack, brow_up, brow_dn,
    bpack_e, bpack_w, bgot_up, bgot_dn, bpgot_up, bpgot_dn,
    send_sem, recv_sem, bsend_sem, brecv_sem,
):
    ty, tx = control.shape[1], control.shape[2]
    ext = ty + 8
    groups = levels // PACK
    lon, lat = lax.axis_index("lon"), lax.axis_index("lat")
    n_lon, n_lat = lax.axis_size("lon"), lax.axis_size("lat")
    east, west = lax.rem(lon + 1, n_lon), lax.rem(lon + n_lon - 1, n_lon)
    has_up, has_dn = lat < n_lat - 1, lat > 0
    columns = (lon, east, west)

    def fetch(src, dst, index):
        return pltpu.make_async_copy(src, dst, local_sem.at[index])

    def fetch_group(g):
        mine = pl.ds(g * PACK, PACK)
        return fetch(control_in.at[mine], control.at[mine], g)

    small = [
        fetch(src, dst, groups + i)
        for i, (src, dst) in enumerate((
            (diffusivity_in, diffusivity), (land_mask_in, land_mask),
            (obs_row_in, obs_row), (obs_col_in, obs_col), (frac_in, frac),
            (innovations_in, innovations), (sigma_in, sigma),
        ))
    ]
    for c in small[:2]:
        c.start()
    for g in range(groups):
        fetch_group(g).start()
    for c in small[2:]:
        c.start()

    barrier = pltpu.get_barrier_semaphore()

    def greet(x, y):
        pl.semaphore_signal(barrier, inc=1, device_id={"lon": x, "lat": y}, device_id_type=MESH)

    greet(east, lat)
    greet(west, lat)

    @pl.when(has_up)
    def _():
        for x in columns:
            greet(x, lat + 1)

    @pl.when(has_dn)
    def _():
        for x in columns:
            greet(x, lat - 1)

    def copy(src, dst, sends, recvs, index, x, y):
        return pltpu.make_async_remote_copy(
            src_ref=src, dst_ref=dst, send_sem=sends.at[index], recv_sem=recvs.at[index],
            device_id={"lon": x, "lat": y}, device_id_type=MESH,
        )

    place = (0, 2, 1)

    lane = lax.broadcasted_iota(jnp.int32, (ext, tx), 1)
    slot = lax.rem(lane, SLOT)
    sub8 = lax.broadcasted_iota(jnp.int32, (8, tx), 0)

    lane_t = lane[0:ty]
    slot_t = slot[0:ty]
    for c in small[:2]:
        c.wait()
    coeff[0] = diffusivity[...]
    coeff[1] = land_mask[...].astype(F32)
    for k in range(2):
        base = jnp.where(lane_t < SLOT, pltpu.roll(coeff[k], 2, 1), 0.0)
        width = SLOT
        while width < tx:
            base = base + pltpu.roll(base, width, 1)
            width *= 2
        pack[groups + k] = base

    def pack_group(g, carry):
        fetch_group(g).wait()
        acc = jnp.zeros((ty, tx), F32)
        for p in range(PACK):
            x = control[g * PACK + p]
            acc = jnp.where(lane_t // SLOT == p, pltpu.roll(x, SLOT * p + 2, 1), acc)
        pack[g] = acc
        return carry

    lax.fori_loop(0, groups, pack_group, 0)
    for q in range(send_e.shape[0]):
        acc = pack[4 * q]
        for j in range(1, min(4, groups + 2 - 4 * q)):
            acc = jnp.where(slot_t // 2 == j, pltpu.roll(pack[4 * q + j], 2 * j, 1), acc)
        send_e[q] = acc
    for q in range(send_w.shape[0]):
        acc = pltpu.roll(pack[2 * q], tx - 2, 1)
        if 2 * q + 1 < groups + 2:
            acc = jnp.where(slot_t < 4, acc, pltpu.roll(pack[2 * q + 1], 2, 1))
        send_w[q] = acc
    rows_up[0:levels] = control[:, ty - EDGE : ty, :]
    rows_dn[0:levels] = control[:, 0:EDGE, :]
    rows_up[levels : levels + 2] = coeff[:, ty - EDGE : ty, :]
    rows_dn[levels : levels + 2] = coeff[:, 0:EDGE, :]
    rows_up[levels + 2 : levels + groups + 4] = pack[:, ty - EDGE : ty, :]
    rows_dn[levels + 2 : levels + groups + 4] = pack[:, 0:EDGE, :]
    packed = pl.ds(levels + 2, groups + 2)

    @pl.when(jnp.logical_and(has_up, has_dn))
    def _():
        pl.semaphore_wait(barrier, 8)

    @pl.when(jnp.logical_not(jnp.logical_and(has_up, has_dn)))
    def _():
        pl.semaphore_wait(barrier, 5)

    side_copies = (
        copy(send_e, from_w, send_sem, recv_sem, 0, east, lat),
        copy(send_w, from_e, send_sem, recv_sem, 1, west, lat),
    )

    def up_copies():
        return [copy(rows_up, got_dn, send_sem, recv_sem, 2, lon, lat + 1)] + [
            copy(rows_up.at[packed], pgot_dn.at[place[i] - 1], send_sem, recv_sem, 3 + i, columns[i], lat + 1)
            for i in (1, 2)
        ]

    def dn_copies():
        return [copy(rows_dn, got_up, send_sem, recv_sem, 3, lon, lat - 1)] + [
            copy(rows_dn.at[packed], pgot_up.at[place[i] - 1], send_sem, recv_sem, 5 + i, columns[i], lat - 1)
            for i in (1, 2)
        ]

    for c in side_copies:
        c.start()

    @pl.when(has_up)
    def _():
        for c in up_copies():
            c.start()

    @pl.when(has_dn)
    def _():
        for c in dn_copies():
            c.start()

    for c in small[2:]:
        c.wait()
    col = obs_col[...]
    row = obs_row[...]
    frac_y = frac[0, 0:1, :]
    frac_x = frac[0, 1:2, :]
    cell = lax.broadcasted_iota(jnp.int32, (tx, tx), 0)
    kind = lax.rem(cell, SLOT)
    picks = jnp.concatenate(
        [jnp.where(col == cell, 1.0, 0.0), jnp.where(col + 1 == cell, 1.0, 0.0)], axis=1
    ).astype(BF16)
    hot_in[0:tx] = picks
    hot_in[tx : 2 * tx] = picks

    def parts(x):
        a = x.astype(BF16)
        rest = x - a.astype(F32)
        b = rest.astype(BF16)
        return a, b, (rest - b.astype(F32)).astype(BF16)

    chosen = jnp.where(
        kind < 3, tx - 2 + kind, jnp.where(kind == 5, 0, jnp.where(kind == 6, 1, jnp.where(kind == 7, 0, -9)))
    )
    for i, wanted in enumerate((cell, chosen)):
        share = jnp.where(col == wanted, 1.0 - frac_x, 0.0) + jnp.where(col + 1 == wanted, frac_x, 0.0)
        high, mid, low = parts(share)
        there = pl.ds(i * tx, tx)
        hot_out[0, there] = jnp.concatenate([high, high], axis=1)
        hot_out[1, there] = jnp.concatenate([mid, mid], axis=1)
        hot_out[2, there] = jnp.concatenate([low, high], axis=1)

    line = lax.broadcasted_iota(jnp.int32, (ext, tx), 0)
    row_weight = jnp.where(line == row, 1.0 - frac_y, 0.0) + jnp.where(line == row + 1, frac_y, 0.0)
    row_weight = jnp.where(jnp.logical_and(line == ty, lat == n_lat - 1), 0.0, row_weight)
    beyond = row_weight * jnp.where(col == tx - 1, frac_x, 0.0)
    live = lax.broadcasted_iota(jnp.int32, (PACK, tx), 1) < counts[0, 0]

    for c in side_copies:
        c.wait()

    @pl.when(has_up)
    def _():
        for c in up_copies():
            c.wait_send()
        for c in dn_copies():
            c.wait_recv()

    @pl.when(has_dn)
    def _():
        for c in dn_copies():
            c.wait_send()
        for c in up_copies():
            c.wait_recv()

    @pl.when(jnp.logical_not(has_up))
    def _():
        got_up[...] = jnp.zeros_like(got_up)
        pgot_up[...] = jnp.zeros_like(pgot_up)

    @pl.when(jnp.logical_not(has_dn))
    def _():
        got_dn[...] = jnp.zeros_like(got_dn)
        pgot_dn[...] = jnp.zeros_like(pgot_dn)

    for k in range(groups + 2):
        q, j = divmod(k, 4)
        pack_w[k] = pltpu.roll(from_w[q], (5 - 2 * j) % tx, 1)
        q, j = divmod(k, 2)
        pack_e[k] = pltpu.roll(from_e[q], tx - 2 if j else 2, 1)

    def strip_of(k):
        at = levels + 2 + k
        own = jnp.concatenate([pack[k], got_up[at], got_dn[at]], axis=0)
        e = jnp.concatenate([pack_e[k], pgot_up[0, k], pgot_dn[0, k]], axis=0)
        w_rows = pltpu.roll(jnp.concatenate([pgot_up[1, k], pgot_dn[1, k]], axis=0), 5, 1)
        w = jnp.concatenate([pack_w[k], w_rows], axis=0)
        far = jnp.where(slot == 7, pltpu.roll(own, 5, 1), w)
        return jnp.where(slot < 2, own, jnp.where(slot < 5, e, far))

    def edge_of(strip):
        return jnp.where(slot == 2, strip, pltpu.roll(strip, tx - 3, 1))

    def around(x, fill):
        left, right = pltpu.roll(x, 1, 1), pltpu.roll(x, tx - 1, 1)
        if fill is not None:
            left = jnp.where(lane == 0, fill, left)
            right = jnp.where(lane == tx - 1, fill, right)
        return left, right, pltpu.roll(x, 1, 0), pltpu.roll(x, ext - 1, 0)

    def fill_of(edge, p):
        return pltpu.roll(edge, (tx - 3 - SLOT * p) % tx, 1)

    def make_weights(dst, kappa, mask, kappas, masks):
        total = jnp.zeros_like(kappa)
        for i in range(4):
            w = 0.5 * (kappa + kappas[i]) * mask * masks[i]
            dst[i] = w
            total = total + w
        dst[4] = 1.0 - total

    kappa_strip, mask_strip = strip_of(groups), strip_of(groups + 1)
    make_weights(
        strip_weights, kappa_strip, mask_strip, around(kappa_strip, None), around(mask_strip, None)
    )
    kappa = jnp.concatenate([coeff[0], got_up[levels], got_dn[levels]], axis=0)
    mask = jnp.concatenate([coeff[1], got_up[levels + 1], got_dn[levels + 1]], axis=0)
    make_weights(
        weights, kappa, mask,
        around(kappa, fill_of(edge_of(kappa_strip), 0)),
        around(mask, fill_of(edge_of(mask_strip), 0)),
    )

    def diffuse(x, fill, w):
        near = around(x, fill)
        out = w[4] * x
        for i in range(4):
            out = out + w[i] * near[i]
        return out

    def dot(x, y, dims, precision=None):
        return lax.dot_general(x, y, (dims, ((), ())), precision=precision, preferred_element_type=F32)

    def back_sides(g):
        return (
            copy(bpack.at[g], bpack_w.at[g], bsend_sem, brecv_sem, g * 8, east, lat),
            copy(bpack.at[g], bpack_e.at[g], bsend_sem, brecv_sem, g * 8 + 1, west, lat),
        )

    def back_up(g):
        return [copy(brow_up.at[g], bgot_dn.at[g], bsend_sem, brecv_sem, g * 8 + 2, lon, lat + 1)] + [
            copy(brow_up.at[g, PACK], bpgot_dn.at[place[i] - 1, g], bsend_sem, brecv_sem, g * 8 + 3 + i, columns[i], lat + 1)
            for i in (1, 2)
        ]

    def back_dn(g):
        return [copy(brow_dn.at[g], bgot_up.at[g], bsend_sem, brecv_sem, g * 8 + 3, lon, lat - 1)] + [
            copy(brow_dn.at[g, PACK], bpgot_up.at[place[i] - 1, g], bsend_sem, brecv_sem, g * 8 + 5 + i, columns[i], lat - 1)
            for i in (1, 2)
        ]

    def forward(g, carry):
        strip0 = strip_of(g)
        edge0 = edge_of(strip0)
        strip1 = diffuse(strip0, None, strip_weights)
        edge1 = edge_of(strip1)
        strip2 = diffuse(strip1, None, strip_weights)
        for p in range(PACK):
            level = g * PACK + p
            x = jnp.concatenate([control[level], got_up[level], got_dn[level]], axis=0)
            x = diffuse(x, fill_of(edge0, p), weights)
            x = diffuse(x, fill_of(edge1, p), weights)
            work[p] = x
        high, mid, low = parts(work[...].reshape(PACK * ext, tx))
        picked = dot(jnp.concatenate([high, mid], axis=1), hot_in[...], ((1,), (0,)))
        picked = picked + dot(low, hot_in[0:tx], ((1,), (0,)))
        outer = dot(strip2, beyond, ((0,), (0,)), lax.Precision.HIGHEST)
        outer = jnp.sum(jnp.where(sub8[None] == 2, outer.reshape(PACK, SLOT, tx), 0.0), axis=1)
        mixed = picked[:, 0:tx] * (1.0 - frac_x) + picked[:, tx : 2 * tx] * frac_x
        sample = jnp.sum(mixed.reshape(PACK, ext, tx) * row_weight[None], axis=1) + outer
        mine = pl.ds(g * PACK, PACK)
        departure = jnp.where(live, sample - innovations[0, mine, :], 0.0)
        departures[0, mine, :] = departure
        s = sigma[0, mine, :]
        weighted = departure / (s * s)
        spread = (weighted[:, None, :] * row_weight[None]).reshape(PACK * ext, tx)
        high, mid, low = parts(spread)
        upper = jnp.concatenate([high, mid], axis=1)
        field = dot(upper, hot_out[0], ((1,), (1,))) + dot(upper, hot_out[1], ((1,), (1,)))
        field = field + dot(jnp.concatenate([high, low], axis=1), hot_out[2], ((1,), (1,)))
        adjoint[mine] = field[:, 0:tx].reshape(PACK, ext, tx)
        sides = field[:, tx : 2 * tx].reshape(PACK, ext, tx)
        acc = sides[0]
        for p in range(1, PACK):
            acc = jnp.where(lane // SLOT == p, sides[p], acc)
        bpack[g] = acc
        brow_up[g, 0:PACK] = adjoint[mine, ty - 3 : ty + 1, :]
        brow_dn[g, 0:PACK] = adjoint[mine, 0:EDGE, :]
        brow_up[g, PACK] = bpack[g, ty - 3 : ty + 1, :]
        brow_dn[g, PACK] = bpack[g, 0:EDGE, :]
        for c in back_sides(g):
            c.start()

        @pl.when(has_up)
        def _():
            for c in back_up(g):
                c.start()

        @pl.when(has_dn)
        def _():
            for c in back_dn(g):
                c.start()

        return carry

    lax.fori_loop(0, groups, forward, 0)

    @pl.when(jnp.logical_not(has_up))
    def _():
        bgot_up[...] = jnp.zeros_like(bgot_up)
        bpgot_up[...] = jnp.zeros_like(bpgot_up)

    @pl.when(jnp.logical_not(has_dn))
    def _():
        bgot_dn[...] = jnp.zeros_like(bgot_dn)
        bpgot_dn[...] = jnp.zeros_like(bpgot_dn)

    def with_rows(x, above, below):
        zero = jnp.zeros((EDGE, tx), F32)
        low = pltpu.roll(jnp.concatenate([zero, below], axis=0), 1, 0)
        first = x[0:8] + jnp.where(sub8 == 0, low, 0.0)
        last = x[ty:ext] + jnp.where(sub8 > 4, low, jnp.concatenate([above, zero], axis=0))
        return jnp.concatenate([first, x[8:ty], last], axis=0)

    def backward(g, carry):
        for c in back_sides(g):
            c.wait()

        @pl.when(has_up)
        def _():
            for c in back_up(g):
                c.wait_send()
            for c in back_dn(g):
                c.wait_recv()

        @pl.when(has_dn)
        def _():
            for c in back_dn(g):
                c.wait_send()
            for c in back_up(g):
                c.wait_recv()

        own = with_rows(bpack[g], bgot_up[g, PACK], bgot_dn[g, PACK])
        e = with_rows(bpack_e[g], bpgot_up[0, g], bpgot_dn[0, g])
        w = with_rows(bpack_w[g], bpgot_up[1, g], bpgot_dn[1, g])
        side_e = pltpu.roll(e, tx - 3, 1)
        side_w = pltpu.roll(w, 5, 1)
        strip = jnp.where(jnp.logical_or(slot < 3, slot == 7), own, 0.0)
        strip = strip + jnp.where(jnp.logical_or(slot == 2, slot == 3), side_e, 0.0)
        strip = strip + jnp.where(slot > 4, side_w, 0.0)
        first_col = jnp.where(slot == 7, side_w, 0.0)
        edge0 = edge_of(strip)
        edge1 = edge_of(diffuse(strip, None, strip_weights))
        for p in range(PACK):
            level = g * PACK + p
            x = with_rows(adjoint[level], bgot_up[g, p], bgot_dn[g, p])
            extra = pltpu.roll(first_col, (tx - 7 - SLOT * p) % tx, 1)
            x = x + jnp.where(lane == 0, extra, 0.0)
            x = diffuse(x, fill_of(edge0, p), weights)
            x = diffuse(x, fill_of(edge1, p), weights)
            gradient[level] = x[0:ty]
        return carry

    lax.fori_loop(0, groups, backward, 0)


def on_device(
    control, diffusivity, land_mask, innovations, obs_sigma, obs_row, obs_col, obs_frac, obs_counts
):
    levels, ty, tx = control.shape
    ext = ty + 8
    groups = levels // PACK
    vmem = pl.BlockSpec(memory_space=pltpu.VMEM)
    smem = pl.BlockSpec(memory_space=pltpu.SMEM)

    def buf(*shape, dtype=F32):
        return pltpu.VMEM(shape, dtype)

    four, two = -(-(groups + 2) // 4), -(-(groups + 2) // 2)
    rows = levels + groups + 4
    scratch = [
        buf(levels, ty, tx), buf(ty, tx), buf(ty, tx, dtype=jnp.int32),
        buf(*innovations.shape), buf(*obs_sigma.shape),
        buf(*obs_row.shape, dtype=jnp.int32), buf(*obs_col.shape, dtype=jnp.int32), buf(*obs_frac.shape),
        pltpu.SemaphoreType.DMA((groups + 7,)),
        buf(2, ty, tx), buf(5, ext, tx), buf(5, ext, tx),
        buf(2 * tx, 2 * tx, dtype=BF16), buf(3, 2 * tx, 2 * tx, dtype=BF16),
        buf(PACK, ext, tx), buf(levels, ext, tx),
        buf(groups + 2, ty, tx), buf(four, ty, tx), buf(two, ty, tx),
        buf(rows, EDGE, tx), buf(rows, EDGE, tx),
        buf(four, ty, tx), buf(two, ty, tx), buf(groups + 2, ty, tx), buf(groups + 2, ty, tx),
        buf(rows, EDGE, tx), buf(rows, EDGE, tx),
        buf(2, groups + 2, EDGE, tx), buf(2, groups + 2, EDGE, tx),
        buf(groups, ext, tx),
        buf(groups, PACK + 1, EDGE, tx), buf(groups, PACK + 1, EDGE, tx),
        buf(groups, ext, tx), buf(groups, ext, tx),
        buf(groups, PACK + 1, EDGE, tx), buf(groups, PACK + 1, EDGE, tx),
        buf(2, groups, EDGE, tx), buf(2, groups, EDGE, tx),
        pltpu.SemaphoreType.DMA((8,)), pltpu.SemaphoreType.DMA((8,)),
        pltpu.SemaphoreType.DMA((8 * groups,)), pltpu.SemaphoreType.DMA((8 * groups,)),
    ]
    return pl.pallas_call(
        functools.partial(kernel, levels),
        out_shape=(
            jax.ShapeDtypeStruct(control.shape, F32),
            jax.ShapeDtypeStruct(innovations.shape, F32),
        ),
        in_specs=[pl.BlockSpec(memory_space=pltpu.HBM)] * 8 + [smem],
        out_specs=(vmem, vmem),
        scratch_shapes=scratch,
        compiler_params=pltpu.CompilerParams(
            collective_id=0, has_side_effects=True, vmem_limit_bytes=40 * 1024 * 1024
        ),
    )(control, diffusivity, land_mask, innovations, obs_sigma, obs_row, obs_col, obs_frac, obs_counts)


def solution(mesh):
    in_specs = (
        P(None, "lat", "lon"),
        P("lat", "lon"),
        P("lat", "lon"),
        P("lat", None, "lon"),
        P("lat", None, "lon"),
        P("lat", "lon"),
        P("lat", "lon"),
        P("lat", None, "lon"),
        P("lat", "lon"),
    )
    out_specs = (P(None, "lat", "lon"), P("lat", None, "lon"))
    return jax.shard_map(
        on_device, mesh=mesh, in_specs=in_specs, out_specs=out_specs, check_vma=False
    )
```

```python
import functools

import jax
import jax.numpy as jnp
from jax import lax
from jax.experimental import pallas as pl
from jax.experimental.pallas import tpu as pltpu
from jax.sharding import PartitionSpec as P

F32 = jnp.float32
BF16 = jnp.bfloat16
PACK = 16
SLOT = 8
EDGE = 4
MESH = pl.DeviceIdType.MESH


def kernel(
    levels,
    control_in, diffusivity_in, land_mask_in, innovations_in, sigma_in,
    obs_row_in, obs_col_in, frac_in, counts,
    gradient, departures,
    control, diffusivity, land_mask, innovations, sigma, obs_row, obs_col, frac, local_sem,
    coeff, weights, strip_weights, hot_in, hot_out, work, adjoint,
    pack, send_e, send_w, rows_up, rows_dn,
    from_w, from_e, pack_e, pack_w, got_up, got_dn, pgot_up, pgot_dn,
    bpack, brow_up, brow_dn,
    bpack_e, bpack_w, bgot_up, bgot_dn, bpgot_up, bpgot_dn,
    send_sem, recv_sem, bsend_sem, brecv_sem,
):
    ty, tx = control.shape[1], control.shape[2]
    ext = ty + 8
    groups = levels // PACK
    lon, lat = lax.axis_index("lon"), lax.axis_index("lat")
    n_lon, n_lat = lax.axis_size("lon"), lax.axis_size("lat")
    east, west = lax.rem(lon + 1, n_lon), lax.rem(lon + n_lon - 1, n_lon)
    has_up, has_dn = lat < n_lat - 1, lat > 0
    columns = (lon, east, west)

    def fetch(src, dst, index):
        return pltpu.make_async_copy(src, dst, local_sem.at[index])

    def fetch_group(g):
        mine = pl.ds(g * PACK, PACK)
        return fetch(control_in.at[mine], control.at[mine], g)

    small = [
        fetch(src, dst, groups + i)
        for i, (src, dst) in enumerate((
            (diffusivity_in, diffusivity), (land_mask_in, land_mask),
            (obs_row_in, obs_row), (obs_col_in, obs_col), (frac_in, frac),
            (innovations_in, innovations), (sigma_in, sigma),
        ))
    ]
    for c in small[:2]:
        c.start()
    for g in range(groups):
        fetch_group(g).start()
    for c in small[2:]:
        c.start()

    barrier = pltpu.get_barrier_semaphore()

    def greet(x, y):
        pl.semaphore_signal(barrier, inc=1, device_id={"lon": x, "lat": y}, device_id_type=MESH)

    greet(east, lat)
    greet(west, lat)

    @pl.when(has_up)
    def _():
        for x in columns:
            greet(x, lat + 1)

    @pl.when(has_dn)
    def _():
        for x in columns:
            greet(x, lat - 1)

    def copy(src, dst, sends, recvs, index, x, y):
        return pltpu.make_async_remote_copy(
            src_ref=src, dst_ref=dst, send_sem=sends.at[index], recv_sem=recvs.at[index],
            device_id={"lon": x, "lat": y}, device_id_type=MESH,
        )

    place = (0, 2, 1)

    lane = lax.broadcasted_iota(jnp.int32, (ext, tx), 1)
    slot = lax.rem(lane, SLOT)
    sub8 = lax.broadcasted_iota(jnp.int32, (8, tx), 0)

    lane_t = lane[0:ty]
    slot_t = slot[0:ty]
    for c in small[:2]:
        c.wait()
    coeff[0] = diffusivity[...]
    coeff[1] = land_mask[...].astype(F32)
    for k in range(2):
        base = jnp.where(lane_t < SLOT, pltpu.roll(coeff[k], 2, 1), 0.0)
        width = SLOT
        while width < tx:
            base = base + pltpu.roll(base, width, 1)
            width *= 2
        pack[groups + k] = base

    def pack_group(g, carry):
        fetch_group(g).wait()
        acc = jnp.zeros((ty, tx), F32)
        for p in range(PACK):
            x = control[g * PACK + p]
            acc = jnp.where(lane_t // SLOT == p, pltpu.roll(x, SLOT * p + 2, 1), acc)
        pack[g] = acc
        return carry

    lax.fori_loop(0, groups, pack_group, 0)
    for q in range(send_e.shape[0]):
        acc = pack[4 * q]
        for j in range(1, min(4, groups + 2 - 4 * q)):
            acc = jnp.where(slot_t // 2 == j, pltpu.roll(pack[4 * q + j], 2 * j, 1), acc)
        send_e[q] = acc
    for q in range(send_w.shape[0]):
        acc = pltpu.roll(pack[2 * q], tx - 2, 1)
        if 2 * q + 1 < groups + 2:
            acc = jnp.where(slot_t < 4, acc, pltpu.roll(pack[2 * q + 1], 2, 1))
        send_w[q] = acc
    rows_up[0:levels] = control[:, ty - EDGE : ty, :]
    rows_dn[0:levels] = control[:, 0:EDGE, :]
    rows_up[levels : levels + 2] = coeff[:, ty - EDGE : ty, :]
    rows_dn[levels : levels + 2] = coeff[:, 0:EDGE, :]
    rows_up[levels + 2 : levels + groups + 4] = pack[:, ty - EDGE : ty, :]
    rows_dn[levels + 2 : levels + groups + 4] = pack[:, 0:EDGE, :]
    packed = pl.ds(levels + 2, groups + 2)

    @pl.when(jnp.logical_and(has_up, has_dn))
    def _():
        pl.semaphore_wait(barrier, 8)

    @pl.when(jnp.logical_not(jnp.logical_and(has_up, has_dn)))
    def _():
        pl.semaphore_wait(barrier, 5)

    side_copies = (
        copy(send_e, from_w, send_sem, recv_sem, 0, east, lat),
        copy(send_w, from_e, send_sem, recv_sem, 1, west, lat),
    )

    def up_copies():
        return [copy(rows_up, got_dn, send_sem, recv_sem, 2, lon, lat + 1)] + [
            copy(rows_up.at[packed], pgot_dn.at[place[i] - 1], send_sem, recv_sem, 3 + i, columns[i], lat + 1)
            for i in (1, 2)
        ]

    def dn_copies():
        return [copy(rows_dn, got_up, send_sem, recv_sem, 3, lon, lat - 1)] + [
            copy(rows_dn.at[packed], pgot_up.at[place[i] - 1], send_sem, recv_sem, 5 + i, columns[i], lat - 1)
            for i in (1, 2)
        ]

    for c in side_copies:
        c.start()

    @pl.when(has_up)
    def _():
        for c in up_copies():
            c.start()

    @pl.when(has_dn)
    def _():
        for c in dn_copies():
            c.start()

    for c in small[2:]:
        c.wait()
    col = obs_col[...]
    row = obs_row[...]
    frac_y = frac[0, 0:1, :]
    frac_x = frac[0, 1:2, :]
    cell = lax.broadcasted_iota(jnp.int32, (tx, tx), 0)
    kind = lax.rem(cell, SLOT)
    picks = jnp.concatenate(
        [jnp.where(col == cell, 1.0, 0.0), jnp.where(col + 1 == cell, 1.0, 0.0)], axis=1
    ).astype(BF16)
    for i in range(3):
        hot_in[i * tx : (i + 1) * tx] = picks

    def parts(x):
        a = x.astype(BF16)
        rest = x - a.astype(F32)
        b = rest.astype(BF16)
        return a, b, (rest - b.astype(F32)).astype(BF16)

    chosen = jnp.where(
        kind < 3, tx - 2 + kind, jnp.where(kind == 5, 0, jnp.where(kind == 6, 1, jnp.where(kind == 7, 0, -9)))
    )
    for i, wanted in enumerate((cell, chosen)):
        share = jnp.where(col == wanted, 1.0 - frac_x, 0.0) + jnp.where(col + 1 == wanted, frac_x, 0.0)
        high, mid, low = parts(share.T)
        for k, part in enumerate((high, high, mid, mid, low, high)):
            hot_out[k * tx : (k + 1) * tx, i * tx : (i + 1) * tx] = part

    line = lax.broadcasted_iota(jnp.int32, (ext, tx), 0)
    row_weight = jnp.where(line == row, 1.0 - frac_y, 0.0) + jnp.where(line == row + 1, frac_y, 0.0)
    row_weight = jnp.where(jnp.logical_and(line == ty, lat == n_lat - 1), 0.0, row_weight)
    beyond = row_weight * jnp.where(col == tx - 1, frac_x, 0.0)
    live = lax.broadcasted_iota(jnp.int32, (PACK, tx), 1) < counts[0, 0]

    for c in side_copies:
        c.wait()

    @pl.when(has_up)
    def _():
        for c in up_copies():
            c.wait_send()
        for c in dn_copies():
            c.wait_recv()

    @pl.when(has_dn)
    def _():
        for c in dn_copies():
            c.wait_send()
        for c in up_copies():
            c.wait_recv()

    @pl.when(jnp.logical_not(has_up))
    def _():
        got_up[...] = jnp.zeros_like(got_up)
        pgot_up[...] = jnp.zeros_like(pgot_up)

    @pl.when(jnp.logical_not(has_dn))
    def _():
        got_dn[...] = jnp.zeros_like(got_dn)
        pgot_dn[...] = jnp.zeros_like(pgot_dn)

    for k in range(groups + 2):
        q, j = divmod(k, 4)
        pack_w[k] = pltpu.roll(from_w[q], (5 - 2 * j) % tx, 1)
        q, j = divmod(k, 2)
        pack_e[k] = pltpu.roll(from_e[q], tx - 2 if j else 2, 1)

    def strip_of(k):
        at = levels + 2 + k
        own = jnp.concatenate([pack[k], got_up[at], got_dn[at]], axis=0)
        e = jnp.concatenate([pack_e[k], pgot_up[0, k], pgot_dn[0, k]], axis=0)
        w_rows = pltpu.roll(jnp.concatenate([pgot_up[1, k], pgot_dn[1, k]], axis=0), 5, 1)
        w = jnp.concatenate([pack_w[k], w_rows], axis=0)
        far = jnp.where(slot == 7, pltpu.roll(own, 5, 1), w)
        return jnp.where(slot < 2, own, jnp.where(slot < 5, e, far))

    def edge_of(strip):
        return jnp.where(slot == 2, strip, pltpu.roll(strip, tx - 3, 1))

    def around(x, fill):
        left, right = pltpu.roll(x, 1, 1), pltpu.roll(x, tx - 1, 1)
        if fill is not None:
            left = jnp.where(lane == 0, fill, left)
            right = jnp.where(lane == tx - 1, fill, right)
        return left, right, pltpu.roll(x, 1, 0), pltpu.roll(x, ext - 1, 0)

    def fill_of(edge, p):
        return pltpu.roll(edge, (tx - 3 - SLOT * p) % tx, 1)

    def make_weights(dst, kappa, mask, kappas, masks):
        total = jnp.zeros_like(kappa)
        for i in range(4):
            w = 0.5 * (kappa + kappas[i]) * mask * masks[i]
            dst[i] = w
            total = total + w
        dst[4] = 1.0 - total

    kappa_strip, mask_strip = strip_of(groups), strip_of(groups + 1)
    make_weights(
        strip_weights, kappa_strip, mask_strip, around(kappa_strip, None), around(mask_strip, None)
    )
    kappa = jnp.concatenate([coeff[0], got_up[levels], got_dn[levels]], axis=0)
    mask = jnp.concatenate([coeff[1], got_up[levels + 1], got_dn[levels + 1]], axis=0)
    make_weights(
        weights, kappa, mask,
        around(kappa, fill_of(edge_of(kappa_strip), 0)),
        around(mask, fill_of(edge_of(mask_strip), 0)),
    )

    def diffuse(x, fill, w):
        near = around(x, fill)
        out = w[4] * x
        for i in range(4):
            out = out + w[i] * near[i]
        return out

    def dot(x, y, dims, precision=None):
        return lax.dot_general(x, y, (dims, ((), ())), precision=precision, preferred_element_type=F32)

    def back_sides(g):
        return (
            copy(bpack.at[g], bpack_w.at[g], bsend_sem, brecv_sem, g * 8, east, lat),
            copy(bpack.at[g], bpack_e.at[g], bsend_sem, brecv_sem, g * 8 + 1, west, lat),
        )

    def back_up(g):
        return [copy(brow_up.at[g], bgot_dn.at[g], bsend_sem, brecv_sem, g * 8 + 2, lon, lat + 1)] + [
            copy(brow_up.at[g, PACK], bpgot_dn.at[place[i] - 1, g], bsend_sem, brecv_sem, g * 8 + 3 + i, columns[i], lat + 1)
            for i in (1, 2)
        ]

    def back_dn(g):
        return [copy(brow_dn.at[g], bgot_up.at[g], bsend_sem, brecv_sem, g * 8 + 3, lon, lat - 1)] + [
            copy(brow_dn.at[g, PACK], bpgot_up.at[place[i] - 1, g], bsend_sem, brecv_sem, g * 8 + 5 + i, columns[i], lat - 1)
            for i in (1, 2)
        ]

    def forward(g, carry):
        strip0 = strip_of(g)
        edge0 = edge_of(strip0)
        strip1 = diffuse(strip0, None, strip_weights)
        edge1 = edge_of(strip1)
        strip2 = diffuse(strip1, None, strip_weights)
        for p in range(0, PACK, 2):
            pair = []
            for q in (p, p + 1):
                level = g * PACK + q
                x = jnp.concatenate([control[level], got_up[level], got_dn[level]], axis=0)
                x = diffuse(x, fill_of(edge0, q), weights)
                pair.append(diffuse(x, fill_of(edge1, q), weights))
            for k, part in enumerate(parts(jnp.concatenate(pair, axis=0))):
                work[p * ext : (p + 2) * ext, k * tx : (k + 1) * tx] = part
        picked = dot(work[...], hot_in[...], ((1,), (0,)))
        outer = dot(strip2, beyond, ((0,), (0,)), lax.Precision.HIGHEST)
        outer = jnp.sum(jnp.where(sub8[None] == 2, outer.reshape(PACK, SLOT, tx), 0.0), axis=1)
        mixed = picked[:, 0:tx] * (1.0 - frac_x) + picked[:, tx : 2 * tx] * frac_x
        sample = jnp.sum(mixed.reshape(PACK, ext, tx) * row_weight[None], axis=1) + outer
        mine = pl.ds(g * PACK, PACK)
        departure = jnp.where(live, sample - innovations[0, mine, :], 0.0)
        departures[0, mine, :] = departure
        s = sigma[0, mine, :]
        weighted = departure / (s * s)
        spread = (weighted[:, None, :] * row_weight[None]).reshape(PACK * ext, tx)
        high, mid, low = parts(spread)
        spread = jnp.concatenate([high, mid, high, mid, high, low], axis=1)
        field = dot(spread, hot_out[...], ((1,), (0,)))
        adjoint[mine] = field[:, 0:tx].reshape(PACK, ext, tx)
        sides = field[:, tx : 2 * tx].reshape(PACK, ext, tx)
        acc = sides[0]
        for p in range(1, PACK):
            acc = jnp.where(lane // SLOT == p, sides[p], acc)
        bpack[g] = acc
        brow_up[g, 0:PACK] = adjoint[mine, ty - 3 : ty + 1, :]
        brow_dn[g, 0:PACK] = adjoint[mine, 0:EDGE, :]
        brow_up[g, PACK] = bpack[g, ty - 3 : ty + 1, :]
        brow_dn[g, PACK] = bpack[g, 0:EDGE, :]
        for c in back_sides(g):
            c.start()

        @pl.when(has_up)
        def _():
            for c in back_up(g):
                c.start()

        @pl.when(has_dn)
        def _():
            for c in back_dn(g):
                c.start()

        return carry

    lax.fori_loop(0, groups, forward, 0)

    @pl.when(jnp.logical_not(has_up))
    def _():
        bgot_up[...] = jnp.zeros_like(bgot_up)
        bpgot_up[...] = jnp.zeros_like(bpgot_up)

    @pl.when(jnp.logical_not(has_dn))
    def _():
        bgot_dn[...] = jnp.zeros_like(bgot_dn)
        bpgot_dn[...] = jnp.zeros_like(bpgot_dn)

    def with_rows(x, above, below):
        zero = jnp.zeros((EDGE, tx), F32)
        low = pltpu.roll(jnp.concatenate([zero, below], axis=0), 1, 0)
        first = x[0:8] + jnp.where(sub8 == 0, low, 0.0)
        last = x[ty:ext] + jnp.where(sub8 > 4, low, jnp.concatenate([above, zero], axis=0))
        return jnp.concatenate([first, x[8:ty], last], axis=0)

    def backward(g, carry):
        for c in back_sides(g):
            c.wait()

        @pl.when(has_up)
        def _():
            for c in back_up(g):
                c.wait_send()
            for c in back_dn(g):
                c.wait_recv()

        @pl.when(has_dn)
        def _():
            for c in back_dn(g):
                c.wait_send()
            for c in back_up(g):
                c.wait_recv()

        own = with_rows(bpack[g], bgot_up[g, PACK], bgot_dn[g, PACK])
        e = with_rows(bpack_e[g], bpgot_up[0, g], bpgot_dn[0, g])
        w = with_rows(bpack_w[g], bpgot_up[1, g], bpgot_dn[1, g])
        side_e = pltpu.roll(e, tx - 3, 1)
        side_w = pltpu.roll(w, 5, 1)
        strip = jnp.where(jnp.logical_or(slot < 3, slot == 7), own, 0.0)
        strip = strip + jnp.where(jnp.logical_or(slot == 2, slot == 3), side_e, 0.0)
        strip = strip + jnp.where(slot > 4, side_w, 0.0)
        first_col = jnp.where(slot == 7, side_w, 0.0)
        edge0 = edge_of(strip)
        edge1 = edge_of(diffuse(strip, None, strip_weights))
        for p in range(PACK):
            level = g * PACK + p
            x = with_rows(adjoint[level], bgot_up[g, p], bgot_dn[g, p])
            extra = pltpu.roll(first_col, (tx - 7 - SLOT * p) % tx, 1)
            x = x + jnp.where(lane == 0, extra, 0.0)
            x = diffuse(x, fill_of(edge0, p), weights)
            x = diffuse(x, fill_of(edge1, p), weights)
            gradient[level] = x[0:ty]
        return carry

    lax.fori_loop(0, groups, backward, 0)


def on_device(
    control, diffusivity, land_mask, innovations, obs_sigma, obs_row, obs_col, obs_frac, obs_counts
):
    levels, ty, tx = control.shape
    ext = ty + 8
    groups = levels // PACK
    vmem = pl.BlockSpec(memory_space=pltpu.VMEM)

    def buf(*shape, dtype=F32):
        return pltpu.VMEM(shape, dtype)

    four, two = -(-(groups + 2) // 4), -(-(groups + 2) // 2)
    rows = levels + groups + 4
    scratch = [
        buf(levels, ty, tx), buf(ty, tx), buf(ty, tx, dtype=jnp.int32),
        buf(*innovations.shape), buf(*obs_sigma.shape),
        buf(*obs_row.shape, dtype=jnp.int32), buf(*obs_col.shape, dtype=jnp.int32), buf(*obs_frac.shape),
        pltpu.SemaphoreType.DMA((groups + 7,)),
        buf(2, ty, tx), buf(5, ext, tx), buf(5, ext, tx),
        buf(3 * tx, 2 * tx, dtype=BF16), buf(6 * tx, 2 * tx, dtype=BF16),
        buf(PACK * ext, 3 * tx, dtype=BF16), buf(levels, ext, tx),
        buf(groups + 2, ty, tx), buf(four, ty, tx), buf(two, ty, tx),
        buf(rows, EDGE, tx), buf(rows, EDGE, tx),
        buf(four, ty, tx), buf(two, ty, tx), buf(groups + 2, ty, tx), buf(groups + 2, ty, tx),
        buf(rows, EDGE, tx), buf(rows, EDGE, tx),
        buf(2, groups + 2, EDGE, tx), buf(2, groups + 2, EDGE, tx),
        buf(groups, ext, tx),
        buf(groups, PACK + 1, EDGE, tx), buf(groups, PACK + 1, EDGE, tx),
        buf(groups, ext, tx), buf(groups, ext, tx),
        buf(groups, PACK + 1, EDGE, tx), buf(groups, PACK + 1, EDGE, tx),
        buf(2, groups, EDGE, tx), buf(2, groups, EDGE, tx),
        pltpu.SemaphoreType.DMA((8,)), pltpu.SemaphoreType.DMA((8,)),
        pltpu.SemaphoreType.DMA((8 * groups,)), pltpu.SemaphoreType.DMA((8 * groups,)),
    ]
    return pl.pallas_call(
        functools.partial(kernel, levels),
        out_shape=(
            jax.ShapeDtypeStruct(control.shape, F32),
            jax.ShapeDtypeStruct(innovations.shape, F32),
        ),
        in_specs=[pl.BlockSpec(memory_space=pltpu.HBM)] * 8 + [pl.BlockSpec(memory_space=pltpu.SMEM)],
        out_specs=(vmem, vmem),
        scratch_shapes=scratch,
        compiler_params=pltpu.CompilerParams(
            collective_id=0, has_side_effects=True, vmem_limit_bytes=40 * 1024 * 1024
        ),
    )(*(
        pltpu.with_memory_space_constraint(a, pltpu.HBM)
        for a in (
            control, diffusivity, land_mask, innovations, obs_sigma, obs_row, obs_col, obs_frac
        )
    ), obs_counts)


def solution(mesh):
    in_specs = (
        P(None, "lat", "lon"),
        P("lat", "lon"),
        P("lat", "lon"),
        P("lat", None, "lon"),
        P("lat", None, "lon"),
        P("lat", "lon"),
        P("lat", "lon"),
        P("lat", None, "lon"),
        P("lat", "lon"),
    )
    out_specs = (P(None, "lat", "lon"), P("lat", None, "lon"))
    return jax.shard_map(
        on_device, mesh=mesh, in_specs=in_specs, out_specs=out_specs, check_vma=False
    )
```

```python
import functools

import jax
import jax.numpy as jnp
from jax import lax
from jax.experimental import pallas as pl
from jax.experimental.pallas import tpu as pltpu
from jax.sharding import PartitionSpec as P

F32 = jnp.float32
BF16 = jnp.bfloat16
PACK = 16
SLOT = 8
EDGE = 4
MESH = pl.DeviceIdType.MESH


def kernel(
    levels,
    control_in, diffusivity_in, land_mask_in, innovations_in, sigma_in,
    obs_row_in, obs_col_in, frac_in, counts,
    gradient, departures,
    control, diffusivity, land_mask, innovations, sigma, obs_row, obs_col, frac, local_sem,
    coeff, weights, strip_weights, hot_in, hot_out, work, shift, adjoint,
    pack, send_e, send_w, rows_up, rows_dn,
    from_w, from_e, pack_e, pack_w, got_up, got_dn, pgot_up, pgot_dn,
    bpack, brow_up, brow_dn,
    bpack_e, bpack_w, bgot_up, bgot_dn, bpgot_up, bpgot_dn,
    send_sem, recv_sem, bsend_sem, brecv_sem,
):
    ty, tx = control.shape[1], control.shape[2]
    ext = ty + 8
    groups = levels // PACK
    lon, lat = lax.axis_index("lon"), lax.axis_index("lat")
    n_lon, n_lat = lax.axis_size("lon"), lax.axis_size("lat")
    east, west = lax.rem(lon + 1, n_lon), lax.rem(lon + n_lon - 1, n_lon)
    has_up, has_dn = lat < n_lat - 1, lat > 0
    columns = (lon, east, west)

    def fetch(src, dst, index):
        return pltpu.make_async_copy(src, dst, local_sem.at[index])

    def fetch_group(g):
        mine = pl.ds(g * PACK, PACK)
        return fetch(control_in.at[mine], control.at[mine], g)

    small = [
        fetch(src, dst, groups + i)
        for i, (src, dst) in enumerate((
            (diffusivity_in, diffusivity), (land_mask_in, land_mask),
            (obs_row_in, obs_row), (obs_col_in, obs_col), (frac_in, frac),
            (innovations_in, innovations), (sigma_in, sigma),
        ))
    ]
    for c in small[:2]:
        c.start()
    for g in range(groups):
        fetch_group(g).start()
    for c in small[2:]:
        c.start()

    barrier = pltpu.get_barrier_semaphore()

    def greet(x, y):
        pl.semaphore_signal(barrier, inc=1, device_id={"lon": x, "lat": y}, device_id_type=MESH)

    greet(east, lat)
    greet(west, lat)

    @pl.when(has_up)
    def _():
        for x in columns:
            greet(x, lat + 1)

    @pl.when(has_dn)
    def _():
        for x in columns:
            greet(x, lat - 1)

    def copy(src, dst, sends, recvs, index, x, y):
        return pltpu.make_async_remote_copy(
            src_ref=src, dst_ref=dst, send_sem=sends.at[index], recv_sem=recvs.at[index],
            device_id={"lon": x, "lat": y}, device_id_type=MESH,
        )

    place = (0, 2, 1)

    lane = lax.broadcasted_iota(jnp.int32, (ext, tx), 1)
    slot = lax.rem(lane, SLOT)
    sub8 = lax.broadcasted_iota(jnp.int32, (8, tx), 0)

    lane_t = lane[0:ty]
    slot_t = slot[0:ty]
    for c in small[:2]:
        c.wait()
    coeff[0] = diffusivity[...]
    coeff[1] = land_mask[...].astype(F32)
    for k in range(2):
        base = jnp.where(lane_t < SLOT, pltpu.roll(coeff[k], 2, 1), 0.0)
        width = SLOT
        while width < tx:
            base = base + pltpu.roll(base, width, 1)
            width *= 2
        pack[groups + k] = base

    def pack_group(g, carry):
        fetch_group(g).wait()
        acc = jnp.zeros((ty, tx), F32)
        for p in range(PACK):
            x = control[g * PACK + p]
            acc = jnp.where(lane_t // SLOT == p, pltpu.roll(x, SLOT * p + 2, 1), acc)
        pack[g] = acc
        return carry

    lax.fori_loop(0, groups, pack_group, 0)
    for q in range(send_e.shape[0]):
        acc = pack[4 * q]
        for j in range(1, min(4, groups + 2 - 4 * q)):
            acc = jnp.where(slot_t // 2 == j, pltpu.roll(pack[4 * q + j], 2 * j, 1), acc)
        send_e[q] = acc
    for q in range(send_w.shape[0]):
        acc = pltpu.roll(pack[2 * q], tx - 2, 1)
        if 2 * q + 1 < groups + 2:
            acc = jnp.where(slot_t < 4, acc, pltpu.roll(pack[2 * q + 1], 2, 1))
        send_w[q] = acc
    rows_up[0:levels] = control[:, ty - EDGE : ty, :]
    rows_dn[0:levels] = control[:, 0:EDGE, :]
    rows_up[levels : levels + 2] = coeff[:, ty - EDGE : ty, :]
    rows_dn[levels : levels + 2] = coeff[:, 0:EDGE, :]
    rows_up[levels + 2 : levels + groups + 4] = pack[:, ty - EDGE : ty, :]
    rows_dn[levels + 2 : levels + groups + 4] = pack[:, 0:EDGE, :]
    packed = pl.ds(levels + 2, groups + 2)

    @pl.when(jnp.logical_and(has_up, has_dn))
    def _():
        pl.semaphore_wait(barrier, 8)

    @pl.when(jnp.logical_not(jnp.logical_and(has_up, has_dn)))
    def _():
        pl.semaphore_wait(barrier, 5)

    side_copies = (
        copy(send_e, from_w, send_sem, recv_sem, 0, east, lat),
        copy(send_w, from_e, send_sem, recv_sem, 1, west, lat),
    )

    def up_copies():
        return [copy(rows_up, got_dn, send_sem, recv_sem, 2, lon, lat + 1)] + [
            copy(rows_up.at[packed], pgot_dn.at[place[i] - 1], send_sem, recv_sem, 3 + i, columns[i], lat + 1)
            for i in (1, 2)
        ]

    def dn_copies():
        return [copy(rows_dn, got_up, send_sem, recv_sem, 3, lon, lat - 1)] + [
            copy(rows_dn.at[packed], pgot_up.at[place[i] - 1], send_sem, recv_sem, 5 + i, columns[i], lat - 1)
            for i in (1, 2)
        ]

    for c in side_copies:
        c.start()

    @pl.when(has_up)
    def _():
        for c in up_copies():
            c.start()

    @pl.when(has_dn)
    def _():
        for c in dn_copies():
            c.start()

    for c in small[2:]:
        c.wait()
    col = obs_col[...]
    row = obs_row[...]
    frac_y = frac[0, 0:1, :]
    frac_x = frac[0, 1:2, :]
    cell = lax.broadcasted_iota(jnp.int32, (tx, tx), 0)
    kind = lax.rem(cell, SLOT)
    picks = jnp.concatenate(
        [jnp.where(col == cell, 1.0, 0.0), jnp.where(col + 1 == cell, 1.0, 0.0)], axis=1
    ).astype(BF16)
    for i in range(3):
        hot_in[i * tx : (i + 1) * tx] = picks

    def parts(x):
        a = x.astype(BF16)
        rest = x - a.astype(F32)
        b = rest.astype(BF16)
        return a, b, (rest - b.astype(F32)).astype(BF16)

    chosen = jnp.where(
        kind < 3, tx - 2 + kind, jnp.where(kind == 5, 0, jnp.where(kind == 6, 1, jnp.where(kind == 7, 0, -9)))
    )
    for i, wanted in enumerate((cell, chosen)):
        share = jnp.where(col == wanted, 1.0 - frac_x, 0.0) + jnp.where(col + 1 == wanted, frac_x, 0.0)
        high, mid, low = parts(share.T)
        for k, part in enumerate((high, high, mid, mid, low, high)):
            hot_out[k * tx : (k + 1) * tx, i * tx : (i + 1) * tx] = part

    line = lax.broadcasted_iota(jnp.int32, (ext, tx), 0)
    row_weight = jnp.where(line == row, 1.0 - frac_y, 0.0) + jnp.where(line == row + 1, frac_y, 0.0)
    row_weight = jnp.where(jnp.logical_and(line == ty, lat == n_lat - 1), 0.0, row_weight)
    beyond = row_weight * jnp.where(col == tx - 1, frac_x, 0.0)
    live = lax.broadcasted_iota(jnp.int32, (PACK, tx), 1) < counts[0, 0]

    for c in side_copies:
        c.wait()

    @pl.when(has_up)
    def _():
        for c in up_copies():
            c.wait_send()
        for c in dn_copies():
            c.wait_recv()

    @pl.when(has_dn)
    def _():
        for c in dn_copies():
            c.wait_send()
        for c in up_copies():
            c.wait_recv()

    @pl.when(jnp.logical_not(has_up))
    def _():
        got_up[...] = jnp.zeros_like(got_up)
        pgot_up[...] = jnp.zeros_like(pgot_up)

    @pl.when(jnp.logical_not(has_dn))
    def _():
        got_dn[...] = jnp.zeros_like(got_dn)
        pgot_dn[...] = jnp.zeros_like(pgot_dn)

    for k in range(groups + 2):
        q, j = divmod(k, 4)
        pack_w[k] = pltpu.roll(from_w[q], (5 - 2 * j) % tx, 1)
        q, j = divmod(k, 2)
        pack_e[k] = pltpu.roll(from_e[q], tx - 2 if j else 2, 1)

    def strip_of(k):
        at = levels + 2 + k
        own = jnp.concatenate([pack[k], got_up[at], got_dn[at]], axis=0)
        e = jnp.concatenate([pack_e[k], pgot_up[0, k], pgot_dn[0, k]], axis=0)
        w_rows = pltpu.roll(jnp.concatenate([pgot_up[1, k], pgot_dn[1, k]], axis=0), 5, 1)
        w = jnp.concatenate([pack_w[k], w_rows], axis=0)
        far = jnp.where(slot == 7, pltpu.roll(own, 5, 1), w)
        return jnp.where(slot < 2, own, jnp.where(slot < 5, e, far))

    def edge_of(strip):
        return jnp.where(slot == 2, strip, pltpu.roll(strip, tx - 3, 1))

    def around(x, fill):
        left, right = pltpu.roll(x, 1, 1), pltpu.roll(x, tx - 1, 1)
        if fill is not None:
            left = jnp.where(lane == 0, fill, left)
            right = jnp.where(lane == tx - 1, fill, right)
        return left, right, pltpu.roll(x, 1, 0), pltpu.roll(x, ext - 1, 0)

    def fill_of(edge, p):
        return pltpu.roll(edge, (tx - 3 - SLOT * p) % tx, 1)

    def make_weights(dst, kappa, mask, kappas, masks):
        total = jnp.zeros_like(kappa)
        for i in range(4):
            w = 0.5 * (kappa + kappas[i]) * mask * masks[i]
            dst[i] = w
            total = total + w
        dst[4] = 1.0 - total

    kappa_strip, mask_strip = strip_of(groups), strip_of(groups + 1)
    make_weights(
        strip_weights, kappa_strip, mask_strip, around(kappa_strip, None), around(mask_strip, None)
    )
    kappa = jnp.concatenate([coeff[0], got_up[levels], got_dn[levels]], axis=0)
    mask = jnp.concatenate([coeff[1], got_up[levels + 1], got_dn[levels + 1]], axis=0)
    make_weights(
        weights, kappa, mask,
        around(kappa, fill_of(edge_of(kappa_strip), 0)),
        around(mask, fill_of(edge_of(mask_strip), 0)),
    )

    def shifted_rows(x, place):
        place[8 : 8 + ext] = x
        place[0:8] = x[ty:ext]
        place[8 + ext : 16 + ext] = x[0:8]
        return place[7 : 7 + ext], place[9 : 9 + ext]

    def diffuse(x, fill, w, place=None):
        if place is None:
            near = around(x, fill)
        else:
            left = jnp.where(lane == 0, fill, pltpu.roll(x, 1, 1))
            right = jnp.where(lane == tx - 1, fill, pltpu.roll(x, tx - 1, 1))
            near = (left, right) + shifted_rows(x, place)
        out = w[4] * x
        for i in range(4):
            out = out + w[i] * near[i]
        return out

    def dot(x, y, dims, precision=None):
        return lax.dot_general(x, y, (dims, ((), ())), precision=precision, preferred_element_type=F32)

    def back_sides(g):
        return (
            copy(bpack.at[g], bpack_w.at[g], bsend_sem, brecv_sem, g * 8, east, lat),
            copy(bpack.at[g], bpack_e.at[g], bsend_sem, brecv_sem, g * 8 + 1, west, lat),
        )

    def back_up(g):
        return [copy(brow_up.at[g], bgot_dn.at[g], bsend_sem, brecv_sem, g * 8 + 2, lon, lat + 1)] + [
            copy(brow_up.at[g, PACK], bpgot_dn.at[place[i] - 1, g], bsend_sem, brecv_sem, g * 8 + 3 + i, columns[i], lat + 1)
            for i in (1, 2)
        ]

    def back_dn(g):
        return [copy(brow_dn.at[g], bgot_up.at[g], bsend_sem, brecv_sem, g * 8 + 3, lon, lat - 1)] + [
            copy(brow_dn.at[g, PACK], bpgot_up.at[place[i] - 1, g], bsend_sem, brecv_sem, g * 8 + 5 + i, columns[i], lat - 1)
            for i in (1, 2)
        ]

    def forward(g, carry):
        strip0 = strip_of(g)
        edge0 = edge_of(strip0)
        strip1 = diffuse(strip0, None, strip_weights)
        edge1 = edge_of(strip1)
        strip2 = diffuse(strip1, None, strip_weights)
        for p in range(0, PACK, 2):
            pair = []
            for q in (p, p + 1):
                level = g * PACK + q
                x = jnp.concatenate([control[level], got_up[level], got_dn[level]], axis=0)
                x = diffuse(x, fill_of(edge0, q), weights, shift.at[q, 0])
                pair.append(diffuse(x, fill_of(edge1, q), weights, shift.at[q, 1]))
            for k, part in enumerate(parts(jnp.concatenate(pair, axis=0))):
                work[p * ext : (p + 2) * ext, k * tx : (k + 1) * tx] = part
        picked = dot(work[...], hot_in[...], ((1,), (0,)))
        outer = dot(strip2, beyond, ((0,), (0,)), lax.Precision.HIGHEST)
        outer = jnp.sum(jnp.where(sub8[None] == 2, outer.reshape(PACK, SLOT, tx), 0.0), axis=1)
        mixed = picked[:, 0:tx] * (1.0 - frac_x) + picked[:, tx : 2 * tx] * frac_x
        sample = jnp.sum(mixed.reshape(PACK, ext, tx) * row_weight[None], axis=1) + outer
        mine = pl.ds(g * PACK, PACK)
        departure = jnp.where(live, sample - innovations[0, mine, :], 0.0)
        departures[0, mine, :] = departure
        s = sigma[0, mine, :]
        weighted = departure / (s * s)
        spread = (weighted[:, None, :] * row_weight[None]).reshape(PACK * ext, tx)
        high, mid, low = parts(spread)
        spread = jnp.concatenate([high, mid, high, mid, high, low], axis=1)
        field = dot(spread, hot_out[...], ((1,), (0,)))
        adjoint[mine] = field[:, 0:tx].reshape(PACK, ext, tx)
        sides = field[:, tx : 2 * tx].reshape(PACK, ext, tx)
        acc = sides[0]
        for p in range(1, PACK):
            acc = jnp.where(lane // SLOT == p, sides[p], acc)
        bpack[g] = acc
        brow_up[g, 0:PACK] = adjoint[mine, ty - 3 : ty + 1, :]
        brow_dn[g, 0:PACK] = adjoint[mine, 0:EDGE, :]
        brow_up[g, PACK] = bpack[g, ty - 3 : ty + 1, :]
        brow_dn[g, PACK] = bpack[g, 0:EDGE, :]
        for c in back_sides(g):
            c.start()

        @pl.when(has_up)
        def _():
            for c in back_up(g):
                c.start()

        @pl.when(has_dn)
        def _():
            for c in back_dn(g):
                c.start()

        return carry

    lax.fori_loop(0, groups, forward, 0)

    @pl.when(jnp.logical_not(has_up))
    def _():
        bgot_up[...] = jnp.zeros_like(bgot_up)
        bpgot_up[...] = jnp.zeros_like(bpgot_up)

    @pl.when(jnp.logical_not(has_dn))
    def _():
        bgot_dn[...] = jnp.zeros_like(bgot_dn)
        bpgot_dn[...] = jnp.zeros_like(bpgot_dn)

    def with_rows(x, above, below):
        zero = jnp.zeros((EDGE, tx), F32)
        low = pltpu.roll(jnp.concatenate([zero, below], axis=0), 1, 0)
        first = x[0:8] + jnp.where(sub8 == 0, low, 0.0)
        last = x[ty:ext] + jnp.where(sub8 > 4, low, jnp.concatenate([above, zero], axis=0))
        return jnp.concatenate([first, x[8:ty], last], axis=0)

    def backward(g, carry):
        for c in back_sides(g):
            c.wait()

        @pl.when(has_up)
        def _():
            for c in back_up(g):
                c.wait_send()
            for c in back_dn(g):
                c.wait_recv()

        @pl.when(has_dn)
        def _():
            for c in back_dn(g):
                c.wait_send()
            for c in back_up(g):
                c.wait_recv()

        own = with_rows(bpack[g], bgot_up[g, PACK], bgot_dn[g, PACK])
        e = with_rows(bpack_e[g], bpgot_up[0, g], bpgot_dn[0, g])
        w = with_rows(bpack_w[g], bpgot_up[1, g], bpgot_dn[1, g])
        side_e = pltpu.roll(e, tx - 3, 1)
        side_w = pltpu.roll(w, 5, 1)
        strip = jnp.where(jnp.logical_or(slot < 3, slot == 7), own, 0.0)
        strip = strip + jnp.where(jnp.logical_or(slot == 2, slot == 3), side_e, 0.0)
        strip = strip + jnp.where(slot > 4, side_w, 0.0)
        first_col = jnp.where(slot == 7, side_w, 0.0)
        edge0 = edge_of(strip)
        edge1 = edge_of(diffuse(strip, None, strip_weights))
        for p in range(PACK):
            level = g * PACK + p
            x = with_rows(adjoint[level], bgot_up[g, p], bgot_dn[g, p])
            extra = pltpu.roll(first_col, (tx - 7 - SLOT * p) % tx, 1)
            x = x + jnp.where(lane == 0, extra, 0.0)
            x = diffuse(x, fill_of(edge0, p), weights, shift.at[p, 0])
            x = diffuse(x, fill_of(edge1, p), weights, shift.at[p, 1])
            gradient[level] = x[0:ty]
        return carry

    lax.fori_loop(0, groups, backward, 0)


def on_device(
    control, diffusivity, land_mask, innovations, obs_sigma, obs_row, obs_col, obs_frac, obs_counts
):
    levels, ty, tx = control.shape
    ext = ty + 8
    groups = levels // PACK
    vmem = pl.BlockSpec(memory_space=pltpu.VMEM)

    def buf(*shape, dtype=F32):
        return pltpu.VMEM(shape, dtype)

    four, two = -(-(groups + 2) // 4), -(-(groups + 2) // 2)
    rows = levels + groups + 4
    scratch = [
        buf(levels, ty, tx), buf(ty, tx), buf(ty, tx, dtype=jnp.int32),
        buf(*innovations.shape), buf(*obs_sigma.shape),
        buf(*obs_row.shape, dtype=jnp.int32), buf(*obs_col.shape, dtype=jnp.int32), buf(*obs_frac.shape),
        pltpu.SemaphoreType.DMA((groups + 7,)),
        buf(2, ty, tx), buf(5, ext, tx), buf(5, ext, tx),
        buf(3 * tx, 2 * tx, dtype=BF16), buf(6 * tx, 2 * tx, dtype=BF16),
        buf(PACK * ext, 3 * tx, dtype=BF16), buf(PACK, 2, ext + 16, tx), buf(levels, ext, tx),
        buf(groups + 2, ty, tx), buf(four, ty, tx), buf(two, ty, tx),
        buf(rows, EDGE, tx), buf(rows, EDGE, tx),
        buf(four, ty, tx), buf(two, ty, tx), buf(groups + 2, ty, tx), buf(groups + 2, ty, tx),
        buf(rows, EDGE, tx), buf(rows, EDGE, tx),
        buf(2, groups + 2, EDGE, tx), buf(2, groups + 2, EDGE, tx),
        buf(groups, ext, tx),
        buf(groups, PACK + 1, EDGE, tx), buf(groups, PACK + 1, EDGE, tx),
        buf(groups, ext, tx), buf(groups, ext, tx),
        buf(groups, PACK + 1, EDGE, tx), buf(groups, PACK + 1, EDGE, tx),
        buf(2, groups, EDGE, tx), buf(2, groups, EDGE, tx),
        pltpu.SemaphoreType.DMA((8,)), pltpu.SemaphoreType.DMA((8,)),
        pltpu.SemaphoreType.DMA((8 * groups,)), pltpu.SemaphoreType.DMA((8 * groups,)),
    ]
    return pl.pallas_call(
        functools.partial(kernel, levels),
        out_shape=(
            jax.ShapeDtypeStruct(control.shape, F32),
            jax.ShapeDtypeStruct(innovations.shape, F32),
        ),
        in_specs=[pl.BlockSpec(memory_space=pltpu.HBM)] * 8 + [pl.BlockSpec(memory_space=pltpu.SMEM)],
        out_specs=(vmem, vmem),
        scratch_shapes=scratch,
        compiler_params=pltpu.CompilerParams(
            collective_id=0, has_side_effects=True, vmem_limit_bytes=40 * 1024 * 1024
        ),
    )(*(
        pltpu.with_memory_space_constraint(a, pltpu.HBM)
        for a in (
            control, diffusivity, land_mask, innovations, obs_sigma, obs_row, obs_col, obs_frac
        )
    ), obs_counts)


def solution(mesh):
    in_specs = (
        P(None, "lat", "lon"),
        P("lat", "lon"),
        P("lat", "lon"),
        P("lat", None, "lon"),
        P("lat", None, "lon"),
        P("lat", "lon"),
        P("lat", "lon"),
        P("lat", None, "lon"),
        P("lat", "lon"),
    )
    out_specs = (P(None, "lat", "lon"), P("lat", None, "lon"))
    return jax.shard_map(
        on_device, mesh=mesh, in_specs=in_specs, out_specs=out_specs, check_vma=False
    )
```

```python
import functools

import jax
import jax.numpy as jnp
from jax import lax
from jax.experimental import pallas as pl
from jax.experimental.pallas import tpu as pltpu
from jax.sharding import PartitionSpec as P

F32 = jnp.float32
BF16 = jnp.bfloat16
PACK = 16
SLOT = 8
EDGE = 4
MESH = pl.DeviceIdType.MESH


def kernel(
    levels,
    control_in, diffusivity_in, land_mask_in, innovations_in, sigma_in,
    obs_row_in, obs_col_in, frac_in, counts,
    gradient, departures,
    control, diffusivity, land_mask, innovations, sigma, obs_row, obs_col, frac, local_sem,
    coeff, weights, strip_weights, hot_in, hot_out, work, adjoint,
    pack, send_e, send_w, rows_up, rows_dn,
    from_w, from_e, pack_e, pack_w, got_up, got_dn, pgot_up, pgot_dn,
    bpack, bsend_e, bsend_w, brow_up, brow_dn,
    bfrom_e, bfrom_w, bpack_e, bpack_w, bgot_up, bgot_dn, bpgot_up, bpgot_dn,
    send_sem, recv_sem, bsend_sem, brecv_sem,
):
    ty, tx = control.shape[1], control.shape[2]
    ext = ty + 8
    groups = levels // PACK
    lon, lat = lax.axis_index("lon"), lax.axis_index("lat")
    n_lon, n_lat = lax.axis_size("lon"), lax.axis_size("lat")
    east, west = lax.rem(lon + 1, n_lon), lax.rem(lon + n_lon - 1, n_lon)
    has_up, has_dn = lat < n_lat - 1, lat > 0
    columns = (lon, east, west)

    def fetch(src, dst, index):
        return pltpu.make_async_copy(src, dst, local_sem.at[index])

    def fetch_group(g):
        mine = pl.ds(g * PACK, PACK)
        return fetch(control_in.at[mine], control.at[mine], g)

    small = [
        fetch(src, dst, groups + i)
        for i, (src, dst) in enumerate((
            (diffusivity_in, diffusivity), (land_mask_in, land_mask),
            (obs_row_in, obs_row), (obs_col_in, obs_col), (frac_in, frac),
            (innovations_in, innovations), (sigma_in, sigma),
        ))
    ]
    for c in small[:2]:
        c.start()
    for g in range(groups):
        fetch_group(g).start()
    for c in small[2:]:
        c.start()

    barrier = pltpu.get_barrier_semaphore()

    def greet(x, y):
        pl.semaphore_signal(barrier, inc=1, device_id={"lon": x, "lat": y}, device_id_type=MESH)

    greet(east, lat)
    greet(west, lat)

    @pl.when(has_up)
    def _():
        for x in columns:
            greet(x, lat + 1)

    @pl.when(has_dn)
    def _():
        for x in columns:
            greet(x, lat - 1)

    def copy(src, dst, sends, recvs, index, x, y):
        return pltpu.make_async_remote_copy(
            src_ref=src, dst_ref=dst, send_sem=sends.at[index], recv_sem=recvs.at[index],
            device_id={"lon": x, "lat": y}, device_id_type=MESH,
        )

    place = (0, 2, 1)

    lane = lax.broadcasted_iota(jnp.int32, (ext, tx), 1)
    slot = lax.rem(lane, SLOT)
    sub8 = lax.broadcasted_iota(jnp.int32, (8, tx), 0)

    lane_t = lane[0:ty]
    slot_t = slot[0:ty]
    for c in small[:2]:
        c.wait()
    coeff[0] = diffusivity[...]
    coeff[1] = land_mask[...].astype(F32)
    for k in range(2):
        base = jnp.where(lane_t < SLOT, pltpu.roll(coeff[k], 2, 1), 0.0)
        width = SLOT
        while width < tx:
            base = base + pltpu.roll(base, width, 1)
            width *= 2
        pack[groups + k] = base

    def pack_group(g, carry):
        fetch_group(g).wait()
        acc = jnp.zeros((ty, tx), F32)
        for p in range(PACK):
            x = control[g * PACK + p]
            acc = jnp.where(lane_t // SLOT == p, pltpu.roll(x, SLOT * p + 2, 1), acc)
        pack[g] = acc
        return carry

    lax.fori_loop(0, groups, pack_group, 0)
    for q in range(send_e.shape[0]):
        acc = pack[4 * q]
        for j in range(1, min(4, groups + 2 - 4 * q)):
            acc = jnp.where(slot_t // 2 == j, pltpu.roll(pack[4 * q + j], 2 * j, 1), acc)
        send_e[q] = acc
    for q in range(send_w.shape[0]):
        acc = pltpu.roll(pack[2 * q], tx - 2, 1)
        if 2 * q + 1 < groups + 2:
            acc = jnp.where(slot_t < 4, acc, pltpu.roll(pack[2 * q + 1], 2, 1))
        send_w[q] = acc
    rows_up[0:levels] = control[:, ty - EDGE : ty, :]
    rows_dn[0:levels] = control[:, 0:EDGE, :]
    rows_up[levels : levels + 2] = coeff[:, ty - EDGE : ty, :]
    rows_dn[levels : levels + 2] = coeff[:, 0:EDGE, :]
    rows_up[levels + 2 : levels + groups + 4] = pack[:, ty - EDGE : ty, :]
    rows_dn[levels + 2 : levels + groups + 4] = pack[:, 0:EDGE, :]
    packed = pl.ds(levels + 2, groups + 2)

    @pl.when(jnp.logical_and(has_up, has_dn))
    def _():
        pl.semaphore_wait(barrier, 8)

    @pl.when(jnp.logical_not(jnp.logical_and(has_up, has_dn)))
    def _():
        pl.semaphore_wait(barrier, 5)

    side_copies = (
        copy(send_e, from_w, send_sem, recv_sem, 0, east, lat),
        copy(send_w, from_e, send_sem, recv_sem, 1, west, lat),
    )

    def up_copies():
        return [copy(rows_up, got_dn, send_sem, recv_sem, 2, lon, lat + 1)] + [
            copy(rows_up.at[packed], pgot_dn.at[place[i] - 1], send_sem, recv_sem, 3 + i, columns[i], lat + 1)
            for i in (1, 2)
        ]

    def dn_copies():
        return [copy(rows_dn, got_up, send_sem, recv_sem, 3, lon, lat - 1)] + [
            copy(rows_dn.at[packed], pgot_up.at[place[i] - 1], send_sem, recv_sem, 5 + i, columns[i], lat - 1)
            for i in (1, 2)
        ]

    for c in side_copies:
        c.start()

    @pl.when(has_up)
    def _():
        for c in up_copies():
            c.start()

    @pl.when(has_dn)
    def _():
        for c in dn_copies():
            c.start()

    for c in small[2:]:
        c.wait()
    col = obs_col[...]
    row = obs_row[...]
    frac_y = frac[0, 0:1, :]
    frac_x = frac[0, 1:2, :]
    cell = lax.broadcasted_iota(jnp.int32, (tx, tx), 0)
    kind = lax.rem(cell, SLOT)
    picks = jnp.concatenate(
        [jnp.where(col == cell, 1.0, 0.0), jnp.where(col + 1 == cell, 1.0, 0.0)], axis=1
    ).astype(BF16)
    for i in range(3):
        hot_in[i * tx : (i + 1) * tx] = picks

    def parts(x):
        a = x.astype(BF16)
        rest = x - a.astype(F32)
        b = rest.astype(BF16)
        return a, b, (rest - b.astype(F32)).astype(BF16)

    chosen = jnp.where(
        kind < 3, tx - 2 + kind, jnp.where(kind == 5, 0, jnp.where(kind == 6, 1, jnp.where(kind == 7, 0, -9)))
    )
    for i, wanted in enumerate((cell, chosen)):
        share = jnp.where(col == wanted, 1.0 - frac_x, 0.0) + jnp.where(col + 1 == wanted, frac_x, 0.0)
        high, mid, low = parts(share.T)
        for k, part in enumerate((high, high, mid, mid, low, high)):
            hot_out[k * tx : (k + 1) * tx, i * tx : (i + 1) * tx] = part

    line = lax.broadcasted_iota(jnp.int32, (ext, tx), 0)
    row_weight = jnp.where(line == row, 1.0 - frac_y, 0.0) + jnp.where(line == row + 1, frac_y, 0.0)
    row_weight = jnp.where(jnp.logical_and(line == ty, lat == n_lat - 1), 0.0, row_weight)
    beyond = row_weight * jnp.where(col == tx - 1, frac_x, 0.0)
    live = lax.broadcasted_iota(jnp.int32, (PACK, tx), 1) < counts[0, 0]

    for c in side_copies:
        c.wait()

    @pl.when(has_up)
    def _():
        for c in up_copies():
            c.wait_send()
        for c in dn_copies():
            c.wait_recv()

    @pl.when(has_dn)
    def _():
        for c in dn_copies():
            c.wait_send()
        for c in up_copies():
            c.wait_recv()

    @pl.when(jnp.logical_not(has_up))
    def _():
        got_up[...] = jnp.zeros_like(got_up)
        pgot_up[...] = jnp.zeros_like(pgot_up)

    @pl.when(jnp.logical_not(has_dn))
    def _():
        got_dn[...] = jnp.zeros_like(got_dn)
        pgot_dn[...] = jnp.zeros_like(pgot_dn)

    for k in range(groups + 2):
        q, j = divmod(k, 4)
        pack_w[k] = pltpu.roll(from_w[q], (5 - 2 * j) % tx, 1)
        q, j = divmod(k, 2)
        pack_e[k] = pltpu.roll(from_e[q], tx - 2 if j else 2, 1)

    def strip_of(k):
        at = levels + 2 + k
        own = jnp.concatenate([pack[k], got_up[at], got_dn[at]], axis=0)
        e = jnp.concatenate([pack_e[k], pgot_up[0, k], pgot_dn[0, k]], axis=0)
        w_rows = pltpu.roll(jnp.concatenate([pgot_up[1, k], pgot_dn[1, k]], axis=0), 5, 1)
        w = jnp.concatenate([pack_w[k], w_rows], axis=0)
        far = jnp.where(slot == 7, pltpu.roll(own, 5, 1), w)
        return jnp.where(slot < 2, own, jnp.where(slot < 5, e, far))

    def edge_of(strip):
        return jnp.where(slot == 2, strip, pltpu.roll(strip, tx - 3, 1))

    def around(x, fill):
        left, right = pltpu.roll(x, 1, 1), pltpu.roll(x, tx - 1, 1)
        if fill is not None:
            left = jnp.where(lane == 0, fill, left)
            right = jnp.where(lane == tx - 1, fill, right)
        return left, right, pltpu.roll(x, 1, 0), pltpu.roll(x, ext - 1, 0)

    def fill_of(edge, p):
        return pltpu.roll(edge, (tx - 3 - SLOT * p) % tx, 1)

    def make_weights(dst, kappa, mask, kappas, masks):
        total = jnp.zeros_like(kappa)
        for i in range(4):
            w = 0.5 * (kappa + kappas[i]) * mask * masks[i]
            dst[i] = w
            total = total + w
        dst[4] = 1.0 - total

    kappa_strip, mask_strip = strip_of(groups), strip_of(groups + 1)
    make_weights(
        strip_weights, kappa_strip, mask_strip, around(kappa_strip, None), around(mask_strip, None)
    )
    kappa = jnp.concatenate([coeff[0], got_up[levels], got_dn[levels]], axis=0)
    mask = jnp.concatenate([coeff[1], got_up[levels + 1], got_dn[levels + 1]], axis=0)
    make_weights(
        weights, kappa, mask,
        around(kappa, fill_of(edge_of(kappa_strip), 0)),
        around(mask, fill_of(edge_of(mask_strip), 0)),
    )

    def diffuse(x, fill, w):
        near = around(x, fill)
        out = w[4] * x
        for i in range(4):
            out = out + w[i] * near[i]
        return out

    def dot(x, y, dims, precision=None):
        return lax.dot_general(x, y, (dims, ((), ())), precision=precision, preferred_element_type=F32)

    cut = (groups + 1) // 2
    chunks = ((0, cut), (cut, groups))

    def back_sides(c):
        lo, hi = chunks[c]
        e, w = pl.ds(0, -(-(hi - lo) // 2)), pl.ds(0, -(-(hi - lo) // 4))
        return (
            copy(bsend_e.at[c, e], bfrom_w.at[c, e], bsend_sem, brecv_sem, c * 8, east, lat),
            copy(bsend_w.at[c, w], bfrom_e.at[c, w], bsend_sem, brecv_sem, c * 8 + 1, west, lat),
        )

    def back_up(c):
        some = pl.ds(chunks[c][0], chunks[c][1] - chunks[c][0])
        return [copy(brow_up.at[some], bgot_dn.at[some], bsend_sem, brecv_sem, c * 8 + 2, lon, lat + 1)] + [
            copy(brow_up.at[some, PACK], bpgot_dn.at[place[i] - 1, some], bsend_sem, brecv_sem, c * 8 + 3 + i, columns[i], lat + 1)
            for i in (1, 2)
        ]

    def back_dn(c):
        some = pl.ds(chunks[c][0], chunks[c][1] - chunks[c][0])
        return [copy(brow_dn.at[some], bgot_up.at[some], bsend_sem, brecv_sem, c * 8 + 3, lon, lat - 1)] + [
            copy(brow_dn.at[some, PACK], bpgot_up.at[place[i] - 1, some], bsend_sem, brecv_sem, c * 8 + 5 + i, columns[i], lat - 1)
            for i in (1, 2)
        ]

    def forward(g, carry):
        strip0 = strip_of(g)
        edge0 = edge_of(strip0)
        strip1 = diffuse(strip0, None, strip_weights)
        edge1 = edge_of(strip1)
        strip2 = diffuse(strip1, None, strip_weights)
        for p in range(0, PACK, 2):
            pair = []
            for q in (p, p + 1):
                level = g * PACK + q
                x = jnp.concatenate([control[level], got_up[level], got_dn[level]], axis=0)
                x = diffuse(x, fill_of(edge0, q), weights)
                pair.append(diffuse(x, fill_of(edge1, q), weights))
            for k, part in enumerate(parts(jnp.concatenate(pair, axis=0))):
                work[p * ext : (p + 2) * ext, k * tx : (k + 1) * tx] = part
        picked = dot(work[...], hot_in[...], ((1,), (0,)))
        outer = dot(strip2, beyond, ((0,), (0,)), lax.Precision.HIGHEST)
        outer = jnp.sum(jnp.where(sub8[None] == 2, outer.reshape(PACK, SLOT, tx), 0.0), axis=1)
        mixed = picked[:, 0:tx] * (1.0 - frac_x) + picked[:, tx : 2 * tx] * frac_x
        sample = jnp.sum(mixed.reshape(PACK, ext, tx) * row_weight[None], axis=1) + outer
        mine = pl.ds(g * PACK, PACK)
        departure = jnp.where(live, sample - innovations[0, mine, :], 0.0)
        departures[0, mine, :] = departure
        s = sigma[0, mine, :]
        weighted = departure / (s * s)
        spread = (weighted[:, None, :] * row_weight[None]).reshape(PACK * ext, tx)
        high, mid, low = parts(spread)
        spread = jnp.concatenate([high, mid, high, mid, high, low], axis=1)
        field = dot(spread, hot_out[...], ((1,), (0,)))
        adjoint[mine] = field[:, 0:tx].reshape(PACK, ext, tx)
        sides = field[:, tx : 2 * tx].reshape(PACK, ext, tx)
        acc = sides[0]
        for p in range(1, PACK):
            acc = jnp.where(lane // SLOT == p, sides[p], acc)
        bpack[g] = acc
        brow_up[g, 0:PACK] = adjoint[mine, ty - 3 : ty + 1, :]
        brow_dn[g, 0:PACK] = adjoint[mine, 0:EDGE, :]
        brow_up[g, PACK] = bpack[g, ty - 3 : ty + 1, :]
        brow_dn[g, PACK] = bpack[g, 0:EDGE, :]
        return carry

    def send_back(c):
        lo, hi = chunks[c]
        for q in range(-(-(hi - lo) // 2)):
            acc = bpack[lo + 2 * q]
            if lo + 2 * q + 1 < hi:
                acc = jnp.where(slot < 4, acc, pltpu.roll(bpack[lo + 2 * q + 1], 4, 1))
            bsend_e[c, q] = acc
        for q in range(-(-(hi - lo) // 4)):
            acc = pltpu.roll(bpack[lo + 4 * q], tx - 5, 1)
            for j in range(1, min(4, hi - lo - 4 * q)):
                acc = jnp.where(slot // 2 == j, pltpu.roll(bpack[lo + 4 * q + j], tx - 5 + 2 * j, 1), acc)
            bsend_w[c, q] = acc
        for d in back_sides(c):
            d.start()

        @pl.when(has_up)
        def _():
            for d in back_up(c):
                d.start()

        @pl.when(has_dn)
        def _():
            for d in back_dn(c):
                d.start()

    for c, (lo, hi) in enumerate(chunks):
        lax.fori_loop(lo, hi, forward, 0)
        send_back(c)

    @pl.when(jnp.logical_not(has_up))
    def _():
        bgot_up[...] = jnp.zeros_like(bgot_up)
        bpgot_up[...] = jnp.zeros_like(bpgot_up)

    @pl.when(jnp.logical_not(has_dn))
    def _():
        bgot_dn[...] = jnp.zeros_like(bgot_dn)
        bpgot_dn[...] = jnp.zeros_like(bpgot_dn)

    def with_rows(x, above, below):
        zero = jnp.zeros((EDGE, tx), F32)
        low = pltpu.roll(jnp.concatenate([zero, below], axis=0), 1, 0)
        first = x[0:8] + jnp.where(sub8 == 0, low, 0.0)
        last = x[ty:ext] + jnp.where(sub8 > 4, low, jnp.concatenate([above, zero], axis=0))
        return jnp.concatenate([first, x[8:ty], last], axis=0)

    def take_back(c):
        for d in back_sides(c):
            d.wait()

        @pl.when(has_up)
        def _():
            for d in back_up(c):
                d.wait_send()
            for d in back_dn(c):
                d.wait_recv()

        @pl.when(has_dn)
        def _():
            for d in back_dn(c):
                d.wait_send()
            for d in back_up(c):
                d.wait_recv()

        for k in range(chunks[c][0], chunks[c][1]):
            q, j = divmod(k - chunks[c][0], 2)
            bpack_w[k] = pltpu.roll(bfrom_w[c, q], 1 if j else 5, 1)
            q, j = divmod(k - chunks[c][0], 4)
            bpack_e[k] = pltpu.roll(bfrom_e[c, q], (2 - 2 * j) % tx, 1)

    def side_of(x, k, g, distance):
        ends = pltpu.roll(jnp.concatenate([bpgot_up[k, g], bpgot_dn[k, g]], axis=0), distance, 1)
        return with_rows(x, ends[0:EDGE], ends[EDGE : 2 * EDGE])

    def backward(g, carry):
        own = with_rows(bpack[g], bgot_up[g, PACK], bgot_dn[g, PACK])
        side_e = side_of(bpack_e[g], 0, g, tx - 3)
        side_w = side_of(bpack_w[g], 1, g, 5)
        strip = jnp.where(jnp.logical_or(slot < 3, slot == 7), own, 0.0)
        strip = strip + jnp.where(jnp.logical_or(slot == 2, slot == 3), side_e, 0.0)
        strip = strip + jnp.where(slot > 4, side_w, 0.0)
        first_col = jnp.where(slot == 7, side_w, 0.0)
        edge0 = edge_of(strip)
        edge1 = edge_of(diffuse(strip, None, strip_weights))
        for p in range(PACK):
            level = g * PACK + p
            x = with_rows(adjoint[level], bgot_up[g, p], bgot_dn[g, p])
            extra = pltpu.roll(first_col, (tx - 7 - SLOT * p) % tx, 1)
            x = x + jnp.where(lane == 0, extra, 0.0)
            x = diffuse(x, fill_of(edge0, p), weights)
            x = diffuse(x, fill_of(edge1, p), weights)
            gradient[level] = x[0:ty]
        return carry

    for c, (lo, hi) in enumerate(chunks):
        take_back(c)
        lax.fori_loop(lo, hi, backward, 0)


def on_device(
    control, diffusivity, land_mask, innovations, obs_sigma, obs_row, obs_col, obs_frac, obs_counts
):
    levels, ty, tx = control.shape
    ext = ty + 8
    groups = levels // PACK
    vmem = pl.BlockSpec(memory_space=pltpu.VMEM)

    def buf(*shape, dtype=F32):
        return pltpu.VMEM(shape, dtype)

    four, two = -(-(groups + 2) // 4), -(-(groups + 2) // 2)
    rows = levels + groups + 4
    half = (groups + 1) // 2
    most_e, most_w = -(-half // 2), -(-half // 4)
    scratch = [
        buf(levels, ty, tx), buf(ty, tx), buf(ty, tx, dtype=jnp.int32),
        buf(*innovations.shape), buf(*obs_sigma.shape),
        buf(*obs_row.shape, dtype=jnp.int32), buf(*obs_col.shape, dtype=jnp.int32), buf(*obs_frac.shape),
        pltpu.SemaphoreType.DMA((groups + 7,)),
        buf(2, ty, tx), buf(5, ext, tx), buf(5, ext, tx),
        buf(3 * tx, 2 * tx, dtype=BF16), buf(6 * tx, 2 * tx, dtype=BF16),
        buf(PACK * ext, 3 * tx, dtype=BF16), buf(levels, ext, tx),
        buf(groups + 2, ty, tx), buf(four, ty, tx), buf(two, ty, tx),
        buf(rows, EDGE, tx), buf(rows, EDGE, tx),
        buf(four, ty, tx), buf(two, ty, tx), buf(groups + 2, ty, tx), buf(groups + 2, ty, tx),
        buf(rows, EDGE, tx), buf(rows, EDGE, tx),
        buf(2, groups + 2, EDGE, tx), buf(2, groups + 2, EDGE, tx),
        buf(groups, ext, tx), buf(2, most_e, ext, tx), buf(2, most_w, ext, tx),
        buf(groups, PACK + 1, EDGE, tx), buf(groups, PACK + 1, EDGE, tx),
        buf(2, most_w, ext, tx), buf(2, most_e, ext, tx),
        buf(groups, ext, tx), buf(groups, ext, tx),
        buf(groups, PACK + 1, EDGE, tx), buf(groups, PACK + 1, EDGE, tx),
        buf(2, groups, EDGE, tx), buf(2, groups, EDGE, tx),
        pltpu.SemaphoreType.DMA((8,)), pltpu.SemaphoreType.DMA((8,)),
        pltpu.SemaphoreType.DMA((16,)), pltpu.SemaphoreType.DMA((16,)),
    ]
    return pl.pallas_call(
        functools.partial(kernel, levels),
        out_shape=(
            jax.ShapeDtypeStruct(control.shape, F32),
            jax.ShapeDtypeStruct(innovations.shape, F32),
        ),
        in_specs=[pl.BlockSpec(memory_space=pltpu.HBM)] * 8 + [pl.BlockSpec(memory_space=pltpu.SMEM)],
        out_specs=(vmem, vmem),
        scratch_shapes=scratch,
        compiler_params=pltpu.CompilerParams(
            collective_id=0, has_side_effects=True, vmem_limit_bytes=40 * 1024 * 1024
        ),
    )(*(
        pltpu.with_memory_space_constraint(a, pltpu.HBM)
        for a in (
            control, diffusivity, land_mask, innovations, obs_sigma, obs_row, obs_col, obs_frac
        )
    ), obs_counts)


def solution(mesh):
    in_specs = (
        P(None, "lat", "lon"),
        P("lat", "lon"),
        P("lat", "lon"),
        P("lat", None, "lon"),
        P("lat", None, "lon"),
        P("lat", "lon"),
        P("lat", "lon"),
        P("lat", None, "lon"),
        P("lat", "lon"),
    )
    out_specs = (P(None, "lat", "lon"), P("lat", None, "lon"))
    return jax.shard_map(
        on_device, mesh=mesh, in_specs=in_specs, out_specs=out_specs, check_vma=False
    )
```

```python
import functools

import jax
import jax.numpy as jnp
from jax import lax
from jax.experimental import pallas as pl
from jax.experimental.pallas import tpu as pltpu
from jax.sharding import PartitionSpec as P

F32 = jnp.float32
BF16 = jnp.bfloat16
PACK = 16
SLOT = 8
EDGE = 4
MESH = pl.DeviceIdType.MESH


def kernel(
    levels,
    control_in, diffusivity_in, land_mask_in, innovations_in, sigma_in,
    obs_row_in, obs_col_in, frac_in, counts,
    gradient, departures,
    control, diffusivity, land_mask, innovations, sigma, obs_row, obs_col, frac, local_sem,
    coeff, weights, strip_weights, hot_in, hot_out, work, adjoint,
    pack, send_e, send_w, rows_up, rows_dn,
    from_w, from_e, pack_e, pack_w, got_up, got_dn, pgot_up, pgot_dn,
    bpack, brow_up, brow_dn,
    bpack_e, bpack_w, bgot_up, bgot_dn, bpgot_up, bpgot_dn,
    send_sem, recv_sem, bsend_sem, brecv_sem,
):
    ty, tx = control.shape[1], control.shape[2]
    ext = ty + 8
    groups = levels // PACK
    lon, lat = lax.axis_index("lon"), lax.axis_index("lat")
    n_lon, n_lat = lax.axis_size("lon"), lax.axis_size("lat")
    east, west = lax.rem(lon + 1, n_lon), lax.rem(lon + n_lon - 1, n_lon)
    has_up, has_dn = lat < n_lat - 1, lat > 0
    columns = (lon, east, west)

    def fetch(src, dst, index):
        return pltpu.make_async_copy(src, dst, local_sem.at[index])

    def fetch_group(g):
        mine = pl.ds(g * PACK, PACK)
        return fetch(control_in.at[mine], control.at[mine], g)

    small = [
        fetch(src, dst, groups + i)
        for i, (src, dst) in enumerate((
            (diffusivity_in, diffusivity), (land_mask_in, land_mask),
            (obs_row_in, obs_row), (obs_col_in, obs_col), (frac_in, frac),
            (innovations_in, innovations), (sigma_in, sigma),
        ))
    ]
    for c in small[:2]:
        c.start()
    for g in range(groups):
        fetch_group(g).start()
    for c in small[2:]:
        c.start()

    barrier = pltpu.get_barrier_semaphore()

    def greet(x, y):
        pl.semaphore_signal(barrier, inc=1, device_id={"lon": x, "lat": y}, device_id_type=MESH)

    greet(east, lat)
    greet(west, lat)

    @pl.when(has_up)
    def _():
        for x in columns:
            greet(x, lat + 1)

    @pl.when(has_dn)
    def _():
        for x in columns:
            greet(x, lat - 1)

    def copy(src, dst, sends, recvs, index, x, y):
        return pltpu.make_async_remote_copy(
            src_ref=src, dst_ref=dst, send_sem=sends.at[index], recv_sem=recvs.at[index],
            device_id={"lon": x, "lat": y}, device_id_type=MESH,
        )

    place = (0, 2, 1)

    lane = lax.broadcasted_iota(jnp.int32, (ext, tx), 1)
    slot = lax.rem(lane, SLOT)
    sub8 = lax.broadcasted_iota(jnp.int32, (8, tx), 0)

    lane_t = lane[0:ty]
    slot_t = slot[0:ty]
    for c in small[:2]:
        c.wait()
    coeff[0] = diffusivity[...]
    coeff[1] = land_mask[...].astype(F32)
    for k in range(2):
        base = jnp.where(lane_t < SLOT, pltpu.roll(coeff[k], 2, 1), 0.0)
        width = SLOT
        while width < tx:
            base = base + pltpu.roll(base, width, 1)
            width *= 2
        pack[groups + k] = base

    def pack_group(g, carry):
        fetch_group(g).wait()

        def some(i, acc):
            for j in range(4):
                p = i * 4 + j
                x = control[g * PACK + p]
                acc = jnp.where(lane_t // SLOT == p, pltpu.roll(x, SLOT * p + 2, 1), acc)
            return acc

        pack[g] = lax.fori_loop(0, PACK // 4, some, jnp.zeros((ty, tx), F32))
        return carry

    lax.fori_loop(0, groups, pack_group, 0)
    for q in range(send_e.shape[0]):
        acc = pack[4 * q]
        for j in range(1, min(4, groups + 2 - 4 * q)):
            acc = jnp.where(slot_t // 2 == j, pltpu.roll(pack[4 * q + j], 2 * j, 1), acc)
        send_e[q] = acc
    for q in range(send_w.shape[0]):
        acc = pltpu.roll(pack[2 * q], tx - 2, 1)
        if 2 * q + 1 < groups + 2:
            acc = jnp.where(slot_t < 4, acc, pltpu.roll(pack[2 * q + 1], 2, 1))
        send_w[q] = acc
    rows_up[0:levels] = control[:, ty - EDGE : ty, :]
    rows_dn[0:levels] = control[:, 0:EDGE, :]
    rows_up[levels : levels + 2] = coeff[:, ty - EDGE : ty, :]
    rows_dn[levels : levels + 2] = coeff[:, 0:EDGE, :]
    rows_up[levels + 2 : levels + groups + 4] = pack[:, ty - EDGE : ty, :]
    rows_dn[levels + 2 : levels + groups + 4] = pack[:, 0:EDGE, :]
    packed = pl.ds(levels + 2, groups + 2)

    @pl.when(jnp.logical_and(has_up, has_dn))
    def _():
        pl.semaphore_wait(barrier, 8)

    @pl.when(jnp.logical_not(jnp.logical_and(has_up, has_dn)))
    def _():
        pl.semaphore_wait(barrier, 5)

    side_copies = (
        copy(send_e, from_w, send_sem, recv_sem, 0, east, lat),
        copy(send_w, from_e, send_sem, recv_sem, 1, west, lat),
    )

    def up_copies():
        return [copy(rows_up, got_dn, send_sem, recv_sem, 2, lon, lat + 1)] + [
            copy(rows_up.at[packed], pgot_dn.at[place[i] - 1], send_sem, recv_sem, 3 + i, columns[i], lat + 1)
            for i in (1, 2)
        ]

    def dn_copies():
        return [copy(rows_dn, got_up, send_sem, recv_sem, 3, lon, lat - 1)] + [
            copy(rows_dn.at[packed], pgot_up.at[place[i] - 1], send_sem, recv_sem, 5 + i, columns[i], lat - 1)
            for i in (1, 2)
        ]

    for c in side_copies:
        c.start()

    @pl.when(has_up)
    def _():
        for c in up_copies():
            c.start()

    @pl.when(has_dn)
    def _():
        for c in dn_copies():
            c.start()

    for c in small[2:]:
        c.wait()
    col = obs_col[...]
    row = obs_row[...]
    frac_y = frac[0, 0:1, :]
    frac_x = frac[0, 1:2, :]
    cell = lax.broadcasted_iota(jnp.int32, (tx, tx), 0)
    kind = lax.rem(cell, SLOT)
    picks = jnp.concatenate(
        [jnp.where(col == cell, 1.0, 0.0), jnp.where(col + 1 == cell, 1.0, 0.0)], axis=1
    ).astype(BF16)
    for i in range(3):
        hot_in[i * tx : (i + 1) * tx] = picks

    def parts(x):
        a = x.astype(BF16)
        rest = x - a.astype(F32)
        b = rest.astype(BF16)
        return a, b, (rest - b.astype(F32)).astype(BF16)

    chosen = jnp.where(
        kind < 3, tx - 2 + kind, jnp.where(kind == 5, 0, jnp.where(kind == 6, 1, jnp.where(kind == 7, 0, -9)))
    )
    for i, wanted in enumerate((cell, chosen)):
        share = jnp.where(col == wanted, 1.0 - frac_x, 0.0) + jnp.where(col + 1 == wanted, frac_x, 0.0)
        high, mid, low = parts(share.T)
        for k, part in enumerate((high, high, mid, mid, low, high)):
            hot_out[k * tx : (k + 1) * tx, i * tx : (i + 1) * tx] = part

    line = lax.broadcasted_iota(jnp.int32, (ext, tx), 0)
    row_weight = jnp.where(line == row, 1.0 - frac_y, 0.0) + jnp.where(line == row + 1, frac_y, 0.0)
    row_weight = jnp.where(jnp.logical_and(line == ty, lat == n_lat - 1), 0.0, row_weight)
    beyond = row_weight * jnp.where(col == tx - 1, frac_x, 0.0)
    live = lax.broadcasted_iota(jnp.int32, (PACK, tx), 1) < counts[0, 0]

    for c in side_copies:
        c.wait()

    @pl.when(has_up)
    def _():
        for c in up_copies():
            c.wait_send()
        for c in dn_copies():
            c.wait_recv()

    @pl.when(has_dn)
    def _():
        for c in dn_copies():
            c.wait_send()
        for c in up_copies():
            c.wait_recv()

    @pl.when(jnp.logical_not(has_up))
    def _():
        got_up[...] = jnp.zeros_like(got_up)
        pgot_up[...] = jnp.zeros_like(pgot_up)

    @pl.when(jnp.logical_not(has_dn))
    def _():
        got_dn[...] = jnp.zeros_like(got_dn)
        pgot_dn[...] = jnp.zeros_like(pgot_dn)

    for k in range(groups + 2):
        q, j = divmod(k, 4)
        pack_w[k] = pltpu.roll(from_w[q], (5 - 2 * j) % tx, 1)
        q, j = divmod(k, 2)
        pack_e[k] = pltpu.roll(from_e[q], tx - 2 if j else 2, 1)

    def strip_of(k):
        at = levels + 2 + k
        own = jnp.concatenate([pack[k], got_up[at], got_dn[at]], axis=0)
        e = jnp.concatenate([pack_e[k], pgot_up[0, k], pgot_dn[0, k]], axis=0)
        w_rows = pltpu.roll(jnp.concatenate([pgot_up[1, k], pgot_dn[1, k]], axis=0), 5, 1)
        w = jnp.concatenate([pack_w[k], w_rows], axis=0)
        far = jnp.where(slot == 7, pltpu.roll(own, 5, 1), w)
        return jnp.where(slot < 2, own, jnp.where(slot < 5, e, far))

    def edge_of(strip):
        return jnp.where(slot == 2, strip, pltpu.roll(strip, tx - 3, 1))

    def around(x, fill):
        left, right = pltpu.roll(x, 1, 1), pltpu.roll(x, tx - 1, 1)
        if fill is not None:
            left = jnp.where(lane == 0, fill, left)
            right = jnp.where(lane == tx - 1, fill, right)
        return left, right, pltpu.roll(x, 1, 0), pltpu.roll(x, ext - 1, 0)

    def fill_of(edge, p):
        return pltpu.roll(edge, lax.rem(2 * tx - 3 - SLOT * p, tx), 1)

    def make_weights(dst, kappa, mask, kappas, masks):
        total = jnp.zeros_like(kappa)
        for i in range(4):
            w = 0.5 * (kappa + kappas[i]) * mask * masks[i]
            dst[i] = w
            total = total + w
        dst[4] = 1.0 - total

    kappa_strip, mask_strip = strip_of(groups), strip_of(groups + 1)
    make_weights(
        strip_weights, kappa_strip, mask_strip, around(kappa_strip, None), around(mask_strip, None)
    )
    kappa = jnp.concatenate([coeff[0], got_up[levels], got_dn[levels]], axis=0)
    mask = jnp.concatenate([coeff[1], got_up[levels + 1], got_dn[levels + 1]], axis=0)
    make_weights(
        weights, kappa, mask,
        around(kappa, fill_of(edge_of(kappa_strip), 0)),
        around(mask, fill_of(edge_of(mask_strip), 0)),
    )

    def diffuse(x, fill, w):
        near = around(x, fill)
        out = w[4] * x
        for i in range(4):
            out = out + w[i] * near[i]
        return out

    def dot(x, y, dims, precision=None):
        return lax.dot_general(x, y, (dims, ((), ())), precision=precision, preferred_element_type=F32)

    def back_sides(g):
        return (
            copy(bpack.at[g], bpack_w.at[g], bsend_sem, brecv_sem, g * 8, east, lat),
            copy(bpack.at[g], bpack_e.at[g], bsend_sem, brecv_sem, g * 8 + 1, west, lat),
        )

    def back_up(g):
        return [copy(brow_up.at[g], bgot_dn.at[g], bsend_sem, brecv_sem, g * 8 + 2, lon, lat + 1)] + [
            copy(brow_up.at[g, PACK], bpgot_dn.at[place[i] - 1, g], bsend_sem, brecv_sem, g * 8 + 3 + i, columns[i], lat + 1)
            for i in (1, 2)
        ]

    def back_dn(g):
        return [copy(brow_dn.at[g], bgot_up.at[g], bsend_sem, brecv_sem, g * 8 + 3, lon, lat - 1)] + [
            copy(brow_dn.at[g, PACK], bpgot_up.at[place[i] - 1, g], bsend_sem, brecv_sem, g * 8 + 5 + i, columns[i], lat - 1)
            for i in (1, 2)
        ]

    def forward(g, carry):
        strip0 = strip_of(g)
        edge0 = edge_of(strip0)
        strip1 = diffuse(strip0, None, strip_weights)
        edge1 = edge_of(strip1)
        strip2 = diffuse(strip1, None, strip_weights)

        def some(i, carry):
            pair = []
            for j in range(2):
                p = i * 2 + j
                level = g * PACK + p
                x = jnp.concatenate([control[level], got_up[level], got_dn[level]], axis=0)
                x = diffuse(x, fill_of(edge0, p), weights)
                pair.append(diffuse(x, fill_of(edge1, p), weights))
            there = pl.ds(pl.multiple_of(i * (2 * ext), 16), 2 * ext)
            for k, part in enumerate(parts(jnp.concatenate(pair, axis=0))):
                work[there, k * tx : (k + 1) * tx] = part
            return carry

        lax.fori_loop(0, PACK // 2, some, 0)
        picked = dot(work[...], hot_in[...], ((1,), (0,)))
        outer = dot(strip2, beyond, ((0,), (0,)), lax.Precision.HIGHEST)
        outer = jnp.sum(jnp.where(sub8[None] == 2, outer.reshape(PACK, SLOT, tx), 0.0), axis=1)
        mixed = picked[:, 0:tx] * (1.0 - frac_x) + picked[:, tx : 2 * tx] * frac_x
        sample = jnp.sum(mixed.reshape(PACK, ext, tx) * row_weight[None], axis=1) + outer
        mine = pl.ds(g * PACK, PACK)
        departure = jnp.where(live, sample - innovations[0, mine, :], 0.0)
        departures[0, mine, :] = departure
        s = sigma[0, mine, :]
        weighted = departure / (s * s)
        spread = (weighted[:, None, :] * row_weight[None]).reshape(PACK * ext, tx)
        high, mid, low = parts(spread)
        spread = jnp.concatenate([high, mid, high, mid, high, low], axis=1)
        field = dot(spread, hot_out[...], ((1,), (0,)))
        adjoint[mine] = field[:, 0:tx].reshape(PACK, ext, tx)
        sides = field[:, tx : 2 * tx].reshape(PACK, ext, tx)
        acc = sides[0]
        for p in range(1, PACK):
            acc = jnp.where(lane // SLOT == p, sides[p], acc)
        bpack[g] = acc
        brow_up[g, 0:PACK] = adjoint[mine, ty - 3 : ty + 1, :]
        brow_dn[g, 0:PACK] = adjoint[mine, 0:EDGE, :]
        brow_up[g, PACK] = bpack[g, ty - 3 : ty + 1, :]
        brow_dn[g, PACK] = bpack[g, 0:EDGE, :]
        for c in back_sides(g):
            c.start()

        @pl.when(has_up)
        def _():
            for c in back_up(g):
                c.start()

        @pl.when(has_dn)
        def _():
            for c in back_dn(g):
                c.start()

        return carry

    lax.fori_loop(0, groups, forward, 0)

    @pl.when(jnp.logical_not(has_up))
    def _():
        bgot_up[...] = jnp.zeros_like(bgot_up)
        bpgot_up[...] = jnp.zeros_like(bpgot_up)

    @pl.when(jnp.logical_not(has_dn))
    def _():
        bgot_dn[...] = jnp.zeros_like(bgot_dn)
        bpgot_dn[...] = jnp.zeros_like(bpgot_dn)

    def with_rows(x, above, below):
        zero = jnp.zeros((EDGE, tx), F32)
        low = pltpu.roll(jnp.concatenate([zero, below], axis=0), 1, 0)
        first = x[0:8] + jnp.where(sub8 == 0, low, 0.0)
        last = x[ty:ext] + jnp.where(sub8 > 4, low, jnp.concatenate([above, zero], axis=0))
        return jnp.concatenate([first, x[8:ty], last], axis=0)

    def backward(g, carry):
        for c in back_sides(g):
            c.wait()

        @pl.when(has_up)
        def _():
            for c in back_up(g):
                c.wait_send()
            for c in back_dn(g):
                c.wait_recv()

        @pl.when(has_dn)
        def _():
            for c in back_dn(g):
                c.wait_send()
            for c in back_up(g):
                c.wait_recv()

        own = with_rows(bpack[g], bgot_up[g, PACK], bgot_dn[g, PACK])
        e = with_rows(bpack_e[g], bpgot_up[0, g], bpgot_dn[0, g])
        w = with_rows(bpack_w[g], bpgot_up[1, g], bpgot_dn[1, g])
        side_e = pltpu.roll(e, tx - 3, 1)
        side_w = pltpu.roll(w, 5, 1)
        strip = jnp.where(jnp.logical_or(slot < 3, slot == 7), own, 0.0)
        strip = strip + jnp.where(jnp.logical_or(slot == 2, slot == 3), side_e, 0.0)
        strip = strip + jnp.where(slot > 4, side_w, 0.0)
        first_col = jnp.where(slot == 7, side_w, 0.0)
        edge0 = edge_of(strip)
        edge1 = edge_of(diffuse(strip, None, strip_weights))

        def some(i, carry):
            for j in range(2):
                p = i * 2 + j
                level = g * PACK + p
                x = with_rows(adjoint[level], bgot_up[g, p], bgot_dn[g, p])
                extra = pltpu.roll(first_col, lax.rem(2 * tx - 7 - SLOT * p, tx), 1)
                x = x + jnp.where(lane == 0, extra, 0.0)
                x = diffuse(x, fill_of(edge0, p), weights)
                x = diffuse(x, fill_of(edge1, p), weights)
                gradient[level] = x[0:ty]
            return carry

        lax.fori_loop(0, PACK // 2, some, 0)
        return carry

    lax.fori_loop(0, groups, backward, 0)


def on_device(
    control, diffusivity, land_mask, innovations, obs_sigma, obs_row, obs_col, obs_frac, obs_counts
):
    levels, ty, tx = control.shape
    ext = ty + 8
    groups = levels // PACK
    vmem = pl.BlockSpec(memory_space=pltpu.VMEM)

    def buf(*shape, dtype=F32):
        return pltpu.VMEM(shape, dtype)

    four, two = -(-(groups + 2) // 4), -(-(groups + 2) // 2)
    rows = levels + groups + 4
    scratch = [
        buf(levels, ty, tx), buf(ty, tx), buf(ty, tx, dtype=jnp.int32),
        buf(*innovations.shape), buf(*obs_sigma.shape),
        buf(*obs_row.shape, dtype=jnp.int32), buf(*obs_col.shape, dtype=jnp.int32), buf(*obs_frac.shape),
        pltpu.SemaphoreType.DMA((groups + 7,)),
        buf(2, ty, tx), buf(5, ext, tx), buf(5, ext, tx),
        buf(3 * tx, 2 * tx, dtype=BF16), buf(6 * tx, 2 * tx, dtype=BF16),
        buf(PACK * ext, 3 * tx, dtype=BF16), buf(levels, ext, tx),
        buf(groups + 2, ty, tx), buf(four, ty, tx), buf(two, ty, tx),
        buf(rows, EDGE, tx), buf(rows, EDGE, tx),
        buf(four, ty, tx), buf(two, ty, tx), buf(groups + 2, ty, tx), buf(groups + 2, ty, tx),
        buf(rows, EDGE, tx), buf(rows, EDGE, tx),
        buf(2, groups + 2, EDGE, tx), buf(2, groups + 2, EDGE, tx),
        buf(groups, ext, tx),
        buf(groups, PACK + 1, EDGE, tx), buf(groups, PACK + 1, EDGE, tx),
        buf(groups, ext, tx), buf(groups, ext, tx),
        buf(groups, PACK + 1, EDGE, tx), buf(groups, PACK + 1, EDGE, tx),
        buf(2, groups, EDGE, tx), buf(2, groups, EDGE, tx),
        pltpu.SemaphoreType.DMA((8,)), pltpu.SemaphoreType.DMA((8,)),
        pltpu.SemaphoreType.DMA((8 * groups,)), pltpu.SemaphoreType.DMA((8 * groups,)),
    ]
    return pl.pallas_call(
        functools.partial(kernel, levels),
        out_shape=(
            jax.ShapeDtypeStruct(control.shape, F32),
            jax.ShapeDtypeStruct(innovations.shape, F32),
        ),
        in_specs=[pl.BlockSpec(memory_space=pltpu.HBM)] * 8 + [pl.BlockSpec(memory_space=pltpu.SMEM)],
        out_specs=(vmem, vmem),
        scratch_shapes=scratch,
        compiler_params=pltpu.CompilerParams(
            collective_id=0, has_side_effects=True, vmem_limit_bytes=40 * 1024 * 1024
        ),
    )(*(
        pltpu.with_memory_space_constraint(a, pltpu.HBM)
        for a in (
            control, diffusivity, land_mask, innovations, obs_sigma, obs_row, obs_col, obs_frac
        )
    ), obs_counts)


def solution(mesh):
    in_specs = (
        P(None, "lat", "lon"),
        P("lat", "lon"),
        P("lat", "lon"),
        P("lat", None, "lon"),
        P("lat", None, "lon"),
        P("lat", "lon"),
        P("lat", "lon"),
        P("lat", None, "lon"),
        P("lat", "lon"),
    )
    out_specs = (P(None, "lat", "lon"), P("lat", None, "lon"))
    return jax.shard_map(
        on_device, mesh=mesh, in_specs=in_specs, out_specs=out_specs, check_vma=False
    )
```

```python
import functools

import jax
import jax.numpy as jnp
from jax import lax
from jax.experimental import pallas as pl
from jax.experimental.pallas import tpu as pltpu
from jax.sharding import PartitionSpec as P

F32 = jnp.float32
BF16 = jnp.bfloat16
PACK = 16
SLOT = 8
EDGE = 4
MESH = pl.DeviceIdType.MESH


def kernel(
    levels,
    control_in, diffusivity_in, land_mask_in, innovations_in, sigma_in,
    obs_row_in, obs_col_in, frac_in, counts,
    gradient, departures,
    control, diffusivity, land_mask, innovations, sigma, obs_row, obs_col, frac, local_sem,
    coeff, weights, strip_weights, hot_in, hot_out, work, adjoint,
    pack, send_e, send_w, rows_up, rows_dn,
    from_w, from_e, pack_e, pack_w, got_up, got_dn, pgot_up, pgot_dn,
    bpack, brow_up, brow_dn,
    bpack_e, bpack_w, bgot_up, bgot_dn, bpgot_up, bpgot_dn,
    send_sem, recv_sem, bsend_sem, brecv_sem,
):
    ty, tx = control.shape[1], control.shape[2]
    ext = ty + 8
    groups = levels // PACK
    lon, lat = lax.axis_index("lon"), lax.axis_index("lat")
    n_lon, n_lat = lax.axis_size("lon"), lax.axis_size("lat")
    east, west = lax.rem(lon + 1, n_lon), lax.rem(lon + n_lon - 1, n_lon)
    has_up, has_dn = lat < n_lat - 1, lat > 0
    columns = (lon, east, west)

    def fetch(src, dst, index):
        return pltpu.make_async_copy(src, dst, local_sem.at[index])

    def fetch_group(g):
        mine = pl.ds(g * PACK, PACK)
        return fetch(control_in.at[mine], control.at[mine], g)

    small = [
        fetch(src, dst, groups + i)
        for i, (src, dst) in enumerate((
            (diffusivity_in, diffusivity), (land_mask_in, land_mask),
            (obs_row_in, obs_row), (obs_col_in, obs_col), (frac_in, frac),
            (innovations_in, innovations), (sigma_in, sigma),
        ))
    ]
    for c in small[:2]:
        c.start()
    for g in range(groups):
        fetch_group(g).start()
    for c in small[2:]:
        c.start()

    barrier = pltpu.get_barrier_semaphore()

    def greet(x, y):
        pl.semaphore_signal(barrier, inc=1, device_id={"lon": x, "lat": y}, device_id_type=MESH)

    greet(east, lat)
    greet(west, lat)

    @pl.when(has_up)
    def _():
        for x in columns:
            greet(x, lat + 1)

    @pl.when(has_dn)
    def _():
        for x in columns:
            greet(x, lat - 1)

    def copy(src, dst, sends, recvs, index, x, y):
        return pltpu.make_async_remote_copy(
            src_ref=src, dst_ref=dst, send_sem=sends.at[index], recv_sem=recvs.at[index],
            device_id={"lon": x, "lat": y}, device_id_type=MESH,
        )

    place = (0, 2, 1)

    lane = lax.broadcasted_iota(jnp.int32, (ext, tx), 1)
    slot = lax.rem(lane, SLOT)
    sub8 = lax.broadcasted_iota(jnp.int32, (8, tx), 0)

    lane_t = lane[0:ty]
    slot_t = slot[0:ty]
    for c in small[:2]:
        c.wait()
    coeff[0] = diffusivity[...]
    coeff[1] = land_mask[...].astype(F32)
    for k in range(2):
        base = jnp.where(lane_t < SLOT, pltpu.roll(coeff[k], 2, 1), 0.0)
        width = SLOT
        while width < tx:
            base = base + pltpu.roll(base, width, 1)
            width *= 2
        pack[groups + k] = base

    def pack_group(g, carry):
        fetch_group(g).wait()
        acc = jnp.zeros((ty, tx), F32)
        for p in range(PACK):
            x = control[g * PACK + p]
            acc = jnp.where(lane_t // SLOT == p, pltpu.roll(x, SLOT * p + 2, 1), acc)
        pack[g] = acc
        return carry

    lax.fori_loop(0, groups, pack_group, 0)
    for q in range(send_e.shape[0]):
        acc = pack[4 * q]
        for j in range(1, min(4, groups + 2 - 4 * q)):
            acc = jnp.where(slot_t // 2 == j, pltpu.roll(pack[4 * q + j], 2 * j, 1), acc)
        send_e[q] = acc
    for q in range(send_w.shape[0]):
        acc = pltpu.roll(pack[2 * q], tx - 2, 1)
        if 2 * q + 1 < groups + 2:
            acc = jnp.where(slot_t < 4, acc, pltpu.roll(pack[2 * q + 1], 2, 1))
        send_w[q] = acc
    rows_up[0:levels] = control[:, ty - EDGE : ty, :]
    rows_dn[0:levels] = control[:, 0:EDGE, :]
    rows_up[levels : levels + 2] = coeff[:, ty - EDGE : ty, :]
    rows_dn[levels : levels + 2] = coeff[:, 0:EDGE, :]
    rows_up[levels + 2 : levels + groups + 4] = pack[:, ty - EDGE : ty, :]
    rows_dn[levels + 2 : levels + groups + 4] = pack[:, 0:EDGE, :]
    packed = pl.ds(levels + 2, groups + 2)

    @pl.when(jnp.logical_and(has_up, has_dn))
    def _():
        pl.semaphore_wait(barrier, 8)

    @pl.when(jnp.logical_not(jnp.logical_and(has_up, has_dn)))
    def _():
        pl.semaphore_wait(barrier, 5)

    side_copies = (
        copy(send_e, from_w, send_sem, recv_sem, 0, east, lat),
        copy(send_w, from_e, send_sem, recv_sem, 1, west, lat),
    )

    def up_copies():
        return [copy(rows_up, got_dn, send_sem, recv_sem, 2, lon, lat + 1)] + [
            copy(rows_up.at[packed], pgot_dn.at[place[i] - 1], send_sem, recv_sem, 3 + i, columns[i], lat + 1)
            for i in (1, 2)
        ]

    def dn_copies():
        return [copy(rows_dn, got_up, send_sem, recv_sem, 3, lon, lat - 1)] + [
            copy(rows_dn.at[packed], pgot_up.at[place[i] - 1], send_sem, recv_sem, 5 + i, columns[i], lat - 1)
            for i in (1, 2)
        ]

    for c in side_copies:
        c.start()

    @pl.when(has_up)
    def _():
        for c in up_copies():
            c.start()

    @pl.when(has_dn)
    def _():
        for c in dn_copies():
            c.start()

    for c in small[2:]:
        c.wait()
    col = obs_col[...]
    row = obs_row[...]
    frac_y = frac[0, 0:1, :]
    frac_x = frac[0, 1:2, :]
    cell = lax.broadcasted_iota(jnp.int32, (tx, tx), 0)
    kind = lax.rem(cell, SLOT)
    picks = jnp.concatenate(
        [jnp.where(col == cell, 1.0, 0.0), jnp.where(col + 1 == cell, 1.0, 0.0)], axis=1
    ).astype(BF16)
    for i in range(3):
        hot_in[i * tx : (i + 1) * tx] = picks

    def parts(x):
        a = x.astype(BF16)
        rest = x - a.astype(F32)
        b = rest.astype(BF16)
        return a, b, (rest - b.astype(F32)).astype(BF16)

    chosen = jnp.where(
        kind < 3, tx - 2 + kind, jnp.where(kind == 5, 0, jnp.where(kind == 6, 1, jnp.where(kind == 7, 0, -9)))
    )
    for i, wanted in enumerate((cell, chosen)):
        share = jnp.where(col == wanted, 1.0 - frac_x, 0.0) + jnp.where(col + 1 == wanted, frac_x, 0.0)
        high, mid, low = parts(share.T)
        for k, part in enumerate((high, high, mid, mid, low, high)):
            hot_out[k * tx : (k + 1) * tx, i * tx : (i + 1) * tx] = part

    line = lax.broadcasted_iota(jnp.int32, (ext, tx), 0)
    row_weight = jnp.where(line == row, 1.0 - frac_y, 0.0) + jnp.where(line == row + 1, frac_y, 0.0)
    row_weight = jnp.where(jnp.logical_and(line == ty, lat == n_lat - 1), 0.0, row_weight)
    beyond = row_weight * jnp.where(col == tx - 1, frac_x, 0.0)
    live = lax.broadcasted_iota(jnp.int32, (PACK, tx), 1) < counts[0, 0]

    for c in side_copies:
        c.wait()

    @pl.when(has_up)
    def _():
        for c in up_copies():
            c.wait_send()
        for c in dn_copies():
            c.wait_recv()

    @pl.when(has_dn)
    def _():
        for c in dn_copies():
            c.wait_send()
        for c in up_copies():
            c.wait_recv()

    @pl.when(jnp.logical_not(has_up))
    def _():
        got_up[...] = jnp.zeros_like(got_up)
        pgot_up[...] = jnp.zeros_like(pgot_up)

    @pl.when(jnp.logical_not(has_dn))
    def _():
        got_dn[...] = jnp.zeros_like(got_dn)
        pgot_dn[...] = jnp.zeros_like(pgot_dn)

    for k in range(groups + 2):
        q, j = divmod(k, 4)
        pack_w[k] = pltpu.roll(from_w[q], (5 - 2 * j) % tx, 1)
        q, j = divmod(k, 2)
        pack_e[k] = pltpu.roll(from_e[q], tx - 2 if j else 2, 1)

    def strip_of(k):
        at = levels + 2 + k
        own = jnp.concatenate([pack[k], got_up[at], got_dn[at]], axis=0)
        e = jnp.concatenate([pack_e[k], pgot_up[0, k], pgot_dn[0, k]], axis=0)
        w_rows = pltpu.roll(jnp.concatenate([pgot_up[1, k], pgot_dn[1, k]], axis=0), 5, 1)
        w = jnp.concatenate([pack_w[k], w_rows], axis=0)
        far = jnp.where(slot == 7, pltpu.roll(own, 5, 1), w)
        return jnp.where(slot < 2, own, jnp.where(slot < 5, e, far))

    def edge_of(strip):
        return jnp.where(slot == 2, strip, pltpu.roll(strip, tx - 3, 1))

    def around(x, fill):
        left, right = pltpu.roll(x, 1, 1), pltpu.roll(x, tx - 1, 1)
        if fill is not None:
            left = jnp.where(lane == 0, fill, left)
            right = jnp.where(lane == tx - 1, fill, right)
        return left, right, pltpu.roll(x, 1, 0), pltpu.roll(x, ext - 1, 0)

    def fill_of(edge, p):
        return pltpu.roll(edge, (tx - 3 - SLOT * p) % tx, 1)

    def make_weights(dst, kappa, mask, kappas, masks):
        total = jnp.zeros_like(kappa)
        for i in range(4):
            w = 0.5 * (kappa + kappas[i]) * mask * masks[i]
            dst[i] = w
            total = total + w
        dst[4] = 1.0 - total

    kappa_strip, mask_strip = strip_of(groups), strip_of(groups + 1)
    make_weights(
        strip_weights, kappa_strip, mask_strip, around(kappa_strip, None), around(mask_strip, None)
    )
    kappa = jnp.concatenate([coeff[0], got_up[levels], got_dn[levels]], axis=0)
    mask = jnp.concatenate([coeff[1], got_up[levels + 1], got_dn[levels + 1]], axis=0)
    make_weights(
        weights, kappa, mask,
        around(kappa, fill_of(edge_of(kappa_strip), 0)),
        around(mask, fill_of(edge_of(mask_strip), 0)),
    )

    def diffuse(x, fill, w):
        near = around(x, fill)
        out = w[4] * x
        for i in range(4):
            out = out + w[i] * near[i]
        return out

    def dot(x, y, dims, precision=None):
        return lax.dot_general(x, y, (dims, ((), ())), precision=precision, preferred_element_type=F32)

    def back_sides(g):
        return (
            copy(bpack.at[g], bpack_w.at[g], bsend_sem, brecv_sem, g * 8, east, lat),
            copy(bpack.at[g], bpack_e.at[g], bsend_sem, brecv_sem, g * 8 + 1, west, lat),
        )

    def back_up(g):
        return [copy(brow_up.at[g], bgot_dn.at[g], bsend_sem, brecv_sem, g * 8 + 2, lon, lat + 1)] + [
            copy(brow_up.at[g, PACK], bpgot_dn.at[place[i] - 1, g], bsend_sem, brecv_sem, g * 8 + 3 + i, columns[i], lat + 1)
            for i in (1, 2)
        ]

    def back_dn(g):
        return [copy(brow_dn.at[g], bgot_up.at[g], bsend_sem, brecv_sem, g * 8 + 3, lon, lat - 1)] + [
            copy(brow_dn.at[g, PACK], bpgot_up.at[place[i] - 1, g], bsend_sem, brecv_sem, g * 8 + 5 + i, columns[i], lat - 1)
            for i in (1, 2)
        ]

    def forward(g, carry):
        strip0 = strip_of(g)
        edge0 = edge_of(strip0)
        strip1 = diffuse(strip0, None, strip_weights)
        edge1 = edge_of(strip1)
        strip2 = diffuse(strip1, None, strip_weights)
        for p in range(0, PACK, 2):
            pair = []
            for q in (p, p + 1):
                level = g * PACK + q
                x = jnp.concatenate([control[level], got_up[level], got_dn[level]], axis=0)
                x = diffuse(x, fill_of(edge0, q), weights)
                pair.append(diffuse(x, fill_of(edge1, q), weights))
            for k, part in enumerate(parts(jnp.concatenate(pair, axis=0))):
                work[p * ext : (p + 2) * ext, k * tx : (k + 1) * tx] = part
        picked = dot(work[...], hot_in[...], ((1,), (0,)))
        outer = dot(strip2, beyond, ((0,), (0,)), lax.Precision.HIGHEST)
        outer = jnp.sum(jnp.where(sub8[None] == 2, outer.reshape(PACK, SLOT, tx), 0.0), axis=1)
        mixed = picked[:, 0:tx] * (1.0 - frac_x) + picked[:, tx : 2 * tx] * frac_x
        sample = jnp.sum(mixed.reshape(PACK, ext, tx) * row_weight[None], axis=1) + outer
        mine = pl.ds(g * PACK, PACK)
        departure = jnp.where(live, sample - innovations[0, mine, :], 0.0)
        departures[0, mine, :] = departure
        s = sigma[0, mine, :]
        weighted = departure / (s * s)
        spread = (weighted[:, None, :] * row_weight[None]).reshape(PACK * ext, tx)
        high, mid, low = parts(spread)
        spread = jnp.concatenate([high, mid, high, mid, high, low], axis=1)
        field = dot(spread, hot_out[...], ((1,), (0,)))
        adjoint[mine] = field[:, 0:tx].reshape(PACK, ext, tx)
        sides = field[:, tx : 2 * tx].reshape(PACK, ext, tx)
        acc = sides[0]
        for p in range(1, PACK):
            acc = jnp.where(lane // SLOT == p, sides[p], acc)
        bpack[g] = acc
        brow_up[g, 0:PACK] = adjoint[mine, ty - 3 : ty + 1, :]
        brow_dn[g, 0:PACK] = adjoint[mine, 0:EDGE, :]
        brow_up[g, PACK] = bpack[g, ty - 3 : ty + 1, :]
        brow_dn[g, PACK] = bpack[g, 0:EDGE, :]
        for c in back_sides(g):
            c.start()

        @pl.when(has_up)
        def _():
            for c in back_up(g):
                c.start()

        @pl.when(has_dn)
        def _():
            for c in back_dn(g):
                c.start()

        return carry

    lax.fori_loop(0, groups, forward, 0)

    @pl.when(jnp.logical_not(has_up))
    def _():
        bgot_up[...] = jnp.zeros_like(bgot_up)
        bpgot_up[...] = jnp.zeros_like(bpgot_up)

    @pl.when(jnp.logical_not(has_dn))
    def _():
        bgot_dn[...] = jnp.zeros_like(bgot_dn)
        bpgot_dn[...] = jnp.zeros_like(bpgot_dn)

    def with_rows(x, above, below):
        zero = jnp.zeros((EDGE, tx), F32)
        low = pltpu.roll(jnp.concatenate([zero, below], axis=0), 1, 0)
        first = x[0:8] + jnp.where(sub8 == 0, low, 0.0)
        last = x[ty:ext] + jnp.where(sub8 > 4, low, jnp.concatenate([above, zero], axis=0))
        return jnp.concatenate([first, x[8:ty], last], axis=0)

    def backward(g, carry):
        for c in back_sides(g):
            c.wait_recv()

        @pl.when(has_up)
        def _():
            for c in back_dn(g):
                c.wait_recv()

        @pl.when(has_dn)
        def _():
            for c in back_up(g):
                c.wait_recv()

        own = with_rows(bpack[g], bgot_up[g, PACK], bgot_dn[g, PACK])
        e = with_rows(bpack_e[g], bpgot_up[0, g], bpgot_dn[0, g])
        w = with_rows(bpack_w[g], bpgot_up[1, g], bpgot_dn[1, g])
        side_e = pltpu.roll(e, tx - 3, 1)
        side_w = pltpu.roll(w, 5, 1)
        strip = jnp.where(jnp.logical_or(slot < 3, slot == 7), own, 0.0)
        strip = strip + jnp.where(jnp.logical_or(slot == 2, slot == 3), side_e, 0.0)
        strip = strip + jnp.where(slot > 4, side_w, 0.0)
        first_col = jnp.where(slot == 7, side_w, 0.0)
        edge0 = edge_of(strip)
        edge1 = edge_of(diffuse(strip, None, strip_weights))
        for p in range(PACK):
            level = g * PACK + p
            x = with_rows(adjoint[level], bgot_up[g, p], bgot_dn[g, p])
            extra = pltpu.roll(first_col, (tx - 7 - SLOT * p) % tx, 1)
            x = x + jnp.where(lane == 0, extra, 0.0)
            x = diffuse(x, fill_of(edge0, p), weights)
            x = diffuse(x, fill_of(edge1, p), weights)
            gradient[level] = x[0:ty]
        return carry

    lax.fori_loop(0, groups, backward, 0)

    def sent(g, carry):
        for c in back_sides(g):
            c.wait_send()

        @pl.when(has_up)
        def _():
            for c in back_up(g):
                c.wait_send()

        @pl.when(has_dn)
        def _():
            for c in back_dn(g):
                c.wait_send()

        return carry

    lax.fori_loop(0, groups, sent, 0)


def on_device(
    control, diffusivity, land_mask, innovations, obs_sigma, obs_row, obs_col, obs_frac, obs_counts
):
    levels, ty, tx = control.shape
    ext = ty + 8
    groups = levels // PACK
    vmem = pl.BlockSpec(memory_space=pltpu.VMEM)

    def buf(*shape, dtype=F32):
        return pltpu.VMEM(shape, dtype)

    four, two = -(-(groups + 2) // 4), -(-(groups + 2) // 2)
    rows = levels + groups + 4
    scratch = [
        buf(levels, ty, tx), buf(ty, tx), buf(ty, tx, dtype=jnp.int32),
        buf(*innovations.shape), buf(*obs_sigma.shape),
        buf(*obs_row.shape, dtype=jnp.int32), buf(*obs_col.shape, dtype=jnp.int32), buf(*obs_frac.shape),
        pltpu.SemaphoreType.DMA((groups + 7,)),
        buf(2, ty, tx), buf(5, ext, tx), buf(5, ext, tx),
        buf(3 * tx, 2 * tx, dtype=BF16), buf(6 * tx, 2 * tx, dtype=BF16),
        buf(PACK * ext, 3 * tx, dtype=BF16), buf(levels, ext, tx),
        buf(groups + 2, ty, tx), buf(four, ty, tx), buf(two, ty, tx),
        buf(rows, EDGE, tx), buf(rows, EDGE, tx),
        buf(four, ty, tx), buf(two, ty, tx), buf(groups + 2, ty, tx), buf(groups + 2, ty, tx),
        buf(rows, EDGE, tx), buf(rows, EDGE, tx),
        buf(2, groups + 2, EDGE, tx), buf(2, groups + 2, EDGE, tx),
        buf(groups, ext, tx),
        buf(groups, PACK + 1, EDGE, tx), buf(groups, PACK + 1, EDGE, tx),
        buf(groups, ext, tx), buf(groups, ext, tx),
        buf(groups, PACK + 1, EDGE, tx), buf(groups, PACK + 1, EDGE, tx),
        buf(2, groups, EDGE, tx), buf(2, groups, EDGE, tx),
        pltpu.SemaphoreType.DMA((8,)), pltpu.SemaphoreType.DMA((8,)),
        pltpu.SemaphoreType.DMA((8 * groups,)), pltpu.SemaphoreType.DMA((8 * groups,)),
    ]
    return pl.pallas_call(
        functools.partial(kernel, levels),
        out_shape=(
            jax.ShapeDtypeStruct(control.shape, F32),
            jax.ShapeDtypeStruct(innovations.shape, F32),
        ),
        in_specs=[pl.BlockSpec(memory_space=pltpu.HBM)] * 8 + [pl.BlockSpec(memory_space=pltpu.SMEM)],
        out_specs=(vmem, vmem),
        scratch_shapes=scratch,
        compiler_params=pltpu.CompilerParams(
            collective_id=0, has_side_effects=True, vmem_limit_bytes=40 * 1024 * 1024
        ),
    )(*(
        pltpu.with_memory_space_constraint(a, pltpu.HBM)
        for a in (
            control, diffusivity, land_mask, innovations, obs_sigma, obs_row, obs_col, obs_frac
        )
    ), obs_counts)


def solution(mesh):
    in_specs = (
        P(None, "lat", "lon"),
        P("lat", "lon"),
        P("lat", "lon"),
        P("lat", None, "lon"),
        P("lat", None, "lon"),
        P("lat", "lon"),
        P("lat", "lon"),
        P("lat", None, "lon"),
        P("lat", "lon"),
    )
    out_specs = (P(None, "lat", "lon"), P("lat", None, "lon"))
    return jax.shard_map(
        on_device, mesh=mesh, in_specs=in_specs, out_specs=out_specs, check_vma=False
    )
```
